512 devices in a mesh: row: 16 (over z_hi, x, core), col: 32 (over z_lo, y).
Axes of the slice: x: 4, y: 8, z: 8 (z_hi: 2, z_lo: 4; z = z_hi * 4 + z_lo), core: 2. Of those that a mesh axis runs over, the one named last changes fastest.
Arguments:
- design: bfloat16 [2048, 14080], P('row', 'col'), may hold values from -0.125 to 0.125
- nuisance_vals: float32 [4, 2048], P(None, 'row'), may hold values from -1 to 1
- arc_index: int32 [2048], P('row'), may hold values from 0 to 63, never falling along the last dimension, each value on 1 to 64 neighbouring positions
- filter_taps: float32 [128], replicated, may hold values from -0.5 to 0.5
- ordering: int32 [14336], replicated, may hold values from 0 to 14335, each once
- normal_prior: float32 [14336, 14336], P('row', 'col'), may hold values from -0.4 to 25
Outputs:
- normal_post: float32 [14336, 14336], P('row', 'col')
The draws below stay inside these ranges and needn't reach their ends.
Inputs may be any that keep to these rules, and one draw needn't show every extreme that they name: `arc_index`: arc numbers never fall along the rows; each arc covers 1 to 64 rows. `ordering`: every slot is the image of exactly one design column.
All inputs are finite; a program needn't handle non-finite values.
Results may differ from the reference program's by a relative error of at most 0.0065.
Values may be sent and summed in bfloat16 or wider, within the bound.
A program may use at most 64 MiB of HBM per device.

```python
import math
import jax
import jax.numpy as jnp
import numpy as np
from jax import lax

COEF = 14080
NPA = 4
NARC = 64
LAG = 128
NUIS = 256
P_SIZE = 14336
OBS = 2048


def draw_normal_prior(key, part):
    base = jax.random.fold_in(key, 7001)
    key_off, key_diag = jax.random.split(base, 2)
    entries = jnp.clip(jax.random.normal(key_off, (P_SIZE, P_SIZE), jnp.float32), -4.0, 4.0)
    off_part = (entries + entries.T) * (0.03 / math.sqrt(2.0))
    diag_part = jax.random.uniform(key_diag, (P_SIZE,), jnp.float32, 2.0, 6.0)
    on_diagonal = jnp.arange(P_SIZE)[:, None] == jnp.arange(P_SIZE)[None, :]
    return jnp.where(on_diagonal, diag_part[:, None] + 0.0 * off_part, off_part)


def steps_of(key, extent, pieces, least, largest):
    loudness, own = 1.0, jax.random.fold_in(key, 6)
    for dim, parts in pieces:
        steps = jnp.exp(jax.random.uniform(jax.random.fold_in(own, dim), (parts,), jnp.float32, least / len(pieces), largest / len(pieces)))
        loudness = loudness * jnp.repeat(steps, extent[dim] // parts).reshape([-1 if axis == dim else 1 for axis in range(len(extent))])
    return loudness


def length_profile(amount, total, most, slope):
    portions = [(1 << 20) // math.isqrt(standing ** slope) + 1 for standing in range(2, amount + 1)]
    surplus, counts = total - most - (amount - 1), [1] * (amount - 1)
    while surplus > 0:
        movable = [i for i in range(amount - 1) if counts[i] < most]
        whole, remaining = sum([portions[i] for i in movable]), surplus
        for i in movable:
            more = min(most - counts[i], max(1, remaining * portions[i] // whole), surplus)
            counts[i] = counts[i] + more
            surplus = surplus - more
    return np.array([most] + counts)


def uneven(own_key, amount, total, reach, lean):
    if amount == 2:
        one = jax.random.randint(own_key, (), max(1, total - reach), min(reach, total - 1) + 1)
        return jnp.stack([one, total - one])
    lengths = jnp.asarray(length_profile(amount, total, reach, lean), jnp.int32)
    twos = (amount - 1) // 2
    giver, receiver = lengths[1:1 + 2 * twos:2], lengths[2:2 + 2 * twos:2]
    slack = jnp.minimum(giver - 1, reach - receiver)
    moved = jax.random.randint(jax.random.fold_in(own_key, 1), (twos,), 0, 1 << 20) % (slack + 1)
    lengths = lengths.at[1:1 + 2 * twos:2].set(giver - moved).at[2:2 + 2 * twos:2].set(receiver + moved)
    return lengths[jax.random.permutation(jax.random.fold_in(own_key, 2), amount)]


def gaussian(rng, extent, width, limit, cuts=(), held_as=jnp.bfloat16):
    result = width * jax.random.normal(rng, extent, jnp.float32)
    if cuts:
        result = result * steps_of(rng, extent, cuts, -0.22, 0.18)
    return jnp.clip(result, -limit, limit).astype(held_as)


def setup_inputs(seed: int = 0) -> dict:
    splits = jax.random.split(jax.random.key(seed), 7)
    return {
        "design": gaussian(splits[0], (OBS, COEF), OBS ** -0.5, 0.125, ((0, 16), (1, 32))),
        "nuisance_vals": gaussian(splits[1], (NPA, OBS), (OBS // NARC) ** -0.5, 1.0, ((1, 16),), jnp.float32),
        "arc_index": jnp.searchsorted(jnp.cumsum(uneven(splits[2], NARC, OBS, 2 * OBS // NARC, 1)), jnp.arange(OBS), side="right").astype(jnp.int32),
        "filter_taps": gaussian(splits[3], (LAG,), LAG ** -0.5, 0.5, (), jnp.float32),
        "ordering": jax.random.permutation(splits[4], P_SIZE).astype(jnp.int32),
        "normal_prior": draw_normal_prior(jax.random.fold_in(splits[6], 71), 0),
    }


def nuisance_block(nuisance_vals, arc_index):
    columns = jnp.arange(NUIS)
    selector = ((columns % NPA)[None, :] == jnp.arange(NPA)[:, None]).astype(jnp.float32)
    picked = jnp.dot(nuisance_vals.T, selector, precision=lax.Precision.HIGHEST, preferred_element_type=jnp.float32)
    return jnp.where(arc_index[:, None] == (columns // NPA)[None, :], picked, jnp.float32(0.0))


def reference(design, nuisance_vals, arc_index, filter_taps, ordering, normal_prior):
    nuisance = nuisance_block(nuisance_vals, arc_index)
    raw = jnp.concatenate([design.astype(jnp.float32), nuisance], 1)
    padded = jnp.concatenate([jnp.zeros((LAG - 1, P_SIZE), jnp.float32), raw], 0)

    def add_lag(step, running):
        start = (LAG - 1 - step).astype(jnp.int32)
        window = lax.dynamic_slice(padded, (start, jnp.int32(0)), (OBS, P_SIZE))
        return running + filter_taps[step] * window

    filtered = lax.fori_loop(0, LAG, add_lag, jnp.zeros((OBS, P_SIZE), jnp.float32)).astype(jnp.bfloat16)
    inverse = jnp.argsort(ordering).astype(jnp.int32)
    ordered = filtered[:, inverse].astype(jnp.float32)
    update = lax.dot_general(ordered, ordered, (((0,), (0,)), ((), ())), preferred_element_type=jnp.float32)
    return normal_prior + update
```

```python
import jax
import jax.numpy as jnp
from jax import lax
from jax.experimental import pallas as pl
from jax.experimental.pallas import tpu as pltpu
from jax.sharding import PartitionSpec as P

MESH = pl.DeviceIdType.MESH
F32, BF16 = jnp.float32, jnp.bfloat16

ROWS, COLS = 16, 32
NPA, NUIS = 4, 256
SEG = 128
COEF_W = 440
TT = 4
RSH, CSH = 896, 448
GROUPS, GTILES = 16, 8


def nt(a, b):
    return lax.dot_general(a, b, (((1,), (1,)), ((), ())), preferred_element_type=F32)


def nn(a, b):
    return lax.dot_general(a, b, (((1,), (0,)), ((), ())), preferred_element_type=F32)


def iota(shape, dim):
    return lax.broadcasted_iota(jnp.int32, shape, dim)


def remote(src, dst, send_sem, recv_sem, row, col):
    return pltpu.make_async_remote_copy(
        src_ref=src,
        dst_ref=dst,
        send_sem=send_sem,
        recv_sem=recv_sem,
        device_id=(row, col),
        device_id_type=MESH,
    )


def kernel(
    design,
    vals,
    arcs,
    taps,
    slots,
    prior,
    out,
    own,
    halo,
    nown,
    nhalo,
    wbuf,
    p1,
    hot_hi,
    hot_lo,
    xg,
    oacc,
    obuf,
    a2,
    b2,
    btw,
    abuf,
    bbuf,
    hsend,
    hrecv,
    psend,
    precv,
    asend,
    arecv,
    bsend,
    brecv,
    gsend,
    grecv,
    qsend,
    qrecv,
    prior_sem,
):
    r, c = lax.axis_index("row"), lax.axis_index("col")
    y, zl0 = c % 8, c // 8
    xi = (r // 2) % 4
    rbase = r - 2 * xi
    r_core = r + 1 - 2 * (r % 2)
    r_z = (r + 8) % ROWS
    r_next, r_prev = (r + 1) % ROWS, (r + ROWS - 1) % ROWS

    def r_x(row, d):
        return row - 2 * xi + 2 * ((xi + d) % 4)

    half, slot_in_half = c // 16, c % 16
    a_col = 2 * r + half
    src_row, src_col = c // 2, 16 * (c % 2)
    is_self = (src_row == r) & (half == c % 2)

    prior_copy = pltpu.make_async_copy(prior, out, prior_sem)
    prior_copy.start()

    barrier = pltpu.get_barrier_semaphore()

    def tell(row, col):
        pl.semaphore_signal(barrier, inc=1, device_id=(row, col), device_id_type=MESH)

    tell(r_prev, c)
    for d in (1, 2, 3):
        tell(r_x(r, d), c)
    tell(r_core, c)
    tell(r_z, c)

    @pl.loop(1, COLS)
    def _(i):
        tell(r, (c + i) % COLS)

    @pl.loop(0, 16)
    def _(i):
        @pl.when(jnp.logical_not(is_self & (i == slot_in_half)))
        def _():
            tell(src_row, src_col + i)

    own[...] = jnp.zeros((512, SEG), BF16)
    own[0:COEF_W, :] = design[...]
    nown[0:4, :] = vals[...]
    nown[4:8, :] = jnp.broadcast_to(arcs[...].astype(F32), (4, SEG))

    pl.semaphore_wait(barrier, 52 + 1 - is_self.astype(jnp.int32))

    halo_copies = [
        remote(own.at[pl.ds(0, 448)], halo.at[pl.ds(0, 448)], hsend.at[0], hrecv.at[0], r_next, c),
        remote(nown, nhalo, hsend.at[1], hrecv.at[1], r_next, c),
    ]
    for copy in halo_copies:
        copy.start()

    hp = (iota((256, 128), 0) // 4).astype(F32)
    lp = iota((256, 128), 0).astype(F32)

    def factors(rows):
        s = rows.astype(F32)
        seg = jnp.floor((s + 0.5) * (1.0 / RSH))
        w = s - seg * RSH
        h = jnp.floor((w + 0.5) * (1.0 / 256.0))
        return jnp.where(rows < 0, -1.0, 4.0 * seg + h), w - 256.0 * h

    def one_hot(row, pattern):
        return jnp.where(jnp.broadcast_to(row, pattern.shape) == pattern, 1.0, 0.0).astype(BF16)

    @pl.loop(0, GROUPS)
    def _(g):
        hi, lo = factors(slots[pl.ds(pl.multiple_of(8 * g, 8), 8), :])
        for i in range(GTILES):
            hot_hi[g, :, 128 * i : 128 * i + 128] = one_hot(hi[i : i + 1], hp)
            hot_lo[g, :, 128 * i : 128 * i + 128] = one_hot(lo[i : i + 1], lp)

    line = jnp.concatenate([taps[...], jnp.zeros((1, SEG), F32)], 1)
    band = pltpu.roll(jnp.broadcast_to(line, (SEG, 2 * SEG)), 0, 1, stride=1, stride_axis=0)
    has_past = jnp.where(r > 0, 1.0, 0.0).astype(F32)
    band_now, band_past = band[:, :SEG], band[:, SEG:] * has_past

    def split(x):
        high = x.astype(BF16)
        return high, (x - high.astype(F32)).astype(BF16)

    now_hi, now_lo = split(band_now)
    past_hi, past_lo = split(band_past)

    for copy in halo_copies:
        copy.wait()

    mine = own[...]
    past = halo[0:448, :]
    filtered = nn(mine, now_hi) + nn(mine, now_lo)
    part = nn(past, past_hi) + nn(past, past_lo)
    filtered = jnp.concatenate([filtered[0:448] + part, filtered[448:512]], 0).astype(BF16)
    p_row, p_time = iota((512, 128), 0), iota((512, 128), 1)
    at_time = p_time == TT * (p_row // 16) + p_row % 4
    wsum = jnp.zeros((512, 128), F32)
    for q in range(4):
        pick = jnp.where(at_time & ((p_row // 4) % 4 == q), 1.0, 0.0).astype(BF16)
        wsum = wsum + nt(pick, filtered[128 * q : 128 * q + 128])
    wbuf[...] = wsum.astype(BF16).reshape(COLS, 16, 128)

    p1[c] = wbuf[c]

    @pl.loop(1, COLS)
    def _(i):
        to = (c + i) % COLS
        remote(wbuf.at[to], p1.at[c], psend.at[i], precv.at[c], r, to).start()

    n_row = iota((NUIS, SEG), 0)

    def nuisance(ref):
        v = jnp.broadcast_to(ref[0:1], (NUIS, SEG))
        for q in range(1, NPA):
            v = jnp.where(n_row % NPA == q, jnp.broadcast_to(ref[q : q + 1], (NUIS, SEG)), v)
        arc = jnp.broadcast_to(ref[4:5], (NUIS, SEG))
        return jnp.where(arc == (n_row // NPA).astype(F32), v, 0.0)

    def exact(a, b):
        return lax.dot_general(
            a, b, (((1,), (0,)), ((), ())), precision=lax.Precision.HIGHEST, preferred_element_type=F32
        )

    nfil = (exact(nuisance(nown), band_now) + exact(nuisance(nhalo), band_past)).astype(BF16)
    s_row, s_time = iota((16, 128), 0), iota((16, 128), 1)
    pick = jnp.where(s_time == TT * c + s_row % 4, 1.0, 0.0).astype(BF16)
    nhi, nlo = factors(slots[128:136, :])
    accum = jnp.zeros((256, 256), F32)
    for q in range(2):
        rep = nt(pick, nfil[128 * q : 128 * q + 128]).astype(BF16)
        x = jnp.concatenate([rep] * 16, 0) * one_hot(nhi[q : q + 1], hp)
        accum = accum + nt(x, one_hot(nlo[q : q + 1], lp))
    oacc[...] = accum

    @pl.loop(1, COLS)
    def _(i):
        src = (c + COLS - i) % COLS
        remote(wbuf.at[src], p1.at[src], psend.at[i], precv.at[src], r, src).wait()

    low4 = iota((8, 128), 0) < 4

    @pl.loop(0, GROUPS)
    def _(g):
        for k in range(2):
            msg = p1[2 * g + k].astype(F32)
            for v in range(2):
                part = msg[8 * v : 8 * v + 8]
                rot = pltpu.roll(part, 4, 0)
                for u in range(2):
                    rep = jnp.where(low4, part, rot) if u == 0 else jnp.where(low4, rot, part)
                    rep = jnp.concatenate([rep, rep], 0).astype(BF16)
                    i = 4 * k + 2 * v + u
                    lanes = slice(128 * i, 128 * i + 128)
                    xg[:, lanes] = jnp.concatenate([rep] * 16, 0) * hot_hi[g, :, lanes]
        oacc[...] += nt(xg[...], hot_lo[g])

    obuf[...] = oacc[...].astype(BF16).reshape(16, 16, 256)

    @pl.loop(0, 16)
    def _(i):
        to = (r + i) % ROWS
        here = is_self & (i == 0)

        @pl.when(here)
        def _():
            a2[slot_in_half] = obuf[r]

        @pl.when(jnp.logical_not(here))
        def _():
            remote(obuf.at[to], a2.at[slot_in_half], asend.at[i], arecv.at[slot_in_half], to, a_col).start()

    b2[c] = obuf[c // 2]

    @pl.loop(1, COLS)
    def _(i):
        to = (c + i) % COLS
        remote(obuf.at[to // 2], b2.at[c], bsend.at[i], brecv.at[c], r, to).start()

    @pl.loop(0, 16)
    def _(i):
        here = is_self & (i == slot_in_half)

        @pl.when(jnp.logical_not(here))
        def _():
            remote(obuf.at[i], a2.at[i], asend.at[i], arecv.at[i], src_row, src_col + i).wait_recv()

    @pl.loop(0, 16)
    def _(i):
        to = (r + i) % ROWS

        @pl.when(jnp.logical_not(is_self & (i == 0)))
        def _():
            remote(obuf.at[to], a2.at[i], asend.at[i], arecv.at[i], to, a_col).wait_send()

    def chunk(zl, yy):
        return abuf.at[zl * 4 + yy // 2, pl.ds(pl.multiple_of(64 * (yy % 2), 64), 64)]

    a_in = a2[...].reshape(256, 256)
    m, p = iota((64, 256), 0), iota((64, 256), 1)
    for h in range(4):
        pick = jnp.where(p == 16 * (m // 4) + 4 * h + m % 4, 1.0, 0.0).astype(BF16)
        width = 256 if h < 3 else 128
        piece = nn(pick, a_in[:, :width]).astype(BF16)
        abuf[c // 2, pl.ds(pl.multiple_of(64 * (c % 2), 64), 64), 256 * h : 256 * h + width] = piece

    y_of = [(y + d) % 8 for d in range(8)]
    zls = [(zl0 + k) % 4 for k in range(4)]
    sends = []

    def pass_on(k, dist, direction):
        yy = y_of[(-direction * dist) % 8]
        n = len(sends)
        copy = remote(
            chunk(zls[k], yy),
            chunk(zls[k], yy),
            gsend.at[n],
            grecv.at[zls[k] * 8 + yy],
            r,
            zl0 * 8 + y_of[direction % 8],
        )
        copy.start()
        sends.append(copy)

    def arrived(zl, yy):
        remote(chunk(zl, yy), chunk(zl, yy), gsend.at[0], grecv.at[zl * 8 + yy], r, c).wait_recv()

    pass_on(0, 0, 1)
    pass_on(0, 0, -1)
    for k in (1, 3, 2):
        copy = remote(
            chunk(zl0, y), chunk(zl0, y), gsend.at[len(sends)], grecv.at[c], r, zls[k] * 8 + y
        )
        copy.start()
        sends.append(copy)

    @pl.loop(1, COLS)
    def _(i):
        src = (c + COLS - i) % COLS
        remote(obuf.at[0], b2.at[src], bsend.at[i], brecv.at[src], r, src).wait()

    b_in = b2[...].reshape(512, 256)
    m, p = iota((128, 512), 0), iota((128, 512), 1)
    for h in range(4):
        pick = jnp.where(p == 16 * (m // 4) + 4 * h + m % 4, 1.0, 0.0).astype(BF16)
        width = 256 if h < 3 else 128
        btw[256 * h : 256 * h + width, :] = nn(pick, b_in[:, :width]).T.astype(BF16)
    bbuf[r] = btw[pl.ds(pl.multiple_of(CSH * (c % 2), 64), CSH), :]

    bsends = []

    def spread(row, to):
        n = len(bsends)
        copy = remote(bbuf.at[row], bbuf.at[row], qsend.at[n], qrecv.at[row], to, c)
        copy.start()
        bsends.append(copy)

    def b_arrived(row):
        remote(bbuf.at[row], bbuf.at[row], qsend.at[0], qrecv.at[row], r, c).wait_recv()

    spread(r, r_z)
    for d in (1, 3, 2):
        spread(r, r_x(r, d))
    spread(r, r_core)

    for k in (1, 3, 2):
        arrived(zls[k], y)
        pass_on(k, 0, 1)
        pass_on(k, 0, -1)

    b_arrived(r_z)
    for d in (1, 3, 2):
        spread(r_z, r_x(r, d))
    spread(r_z, r_core)

    def product(k, pair):
        idx = zls[k] * 4 + pair
        out[...] += nn(bbuf[idx], abuf[idx])

    pair0 = y // 2
    for s in range(1, 5):
        for k in range(4):
            right, left = (4, 3) if k % 2 == 0 else (3, 4)
            if s <= right:
                arrived(zls[k], y_of[-s % 8])
                if s < right:
                    pass_on(k, s, 1)
            if s <= left:
                arrived(zls[k], y_of[s % 8])
                if s < left:
                    pass_on(k, s, -1)
            if s == 2:
                product(k, pair0)
            if s == 3:
                product(k, (pair0 + 1) % 4)
                product(k, (pair0 + 3) % 4)
            if s == 4:
                product(k, (pair0 + 2) % 4)
        if s == 1:
            for base in (r, r_z):
                for d in (1, 3, 2):
                    b_arrived(r_x(base, d))
                    spread(r_x(base, d), r_core)
            for base in (r, r_z):
                for d in range(4):
                    row = r_x(base, d)
                    b_arrived(row + 1 - 2 * (row % 2))
            prior_copy.wait()

    for copy in sends + bsends:
        copy.wait_send()


def per_device(design, nuisance_vals, arc_index, filter_taps, ordering, normal_prior):
    coef = COEF_W * COLS
    cols = jnp.pad(ordering[:coef].reshape(COLS, COEF_W), ((0, 0), (0, 512 - COEF_W)), constant_values=-1)
    slots = jnp.concatenate(
        [cols.reshape(128, 128), ordering[coef:].reshape(2, 128), jnp.full((6, 128), -1, jnp.int32)], 0
    )
    vmem = pl.BlockSpec(memory_space=pltpu.VMEM)
    dma = pltpu.SemaphoreType.DMA
    result = pl.pallas_call(
        kernel,
        out_shape=jax.ShapeDtypeStruct((CSH, RSH), F32),
        in_specs=[vmem] * 5 + [pl.BlockSpec(memory_space=pl.ANY)],
        out_specs=vmem,
        scratch_shapes=[
            pltpu.VMEM((512, SEG), BF16),
            pltpu.VMEM((512, SEG), BF16),
            pltpu.VMEM((8, SEG), F32),
            pltpu.VMEM((8, SEG), F32),
            pltpu.VMEM((COLS, 16, 128), BF16),
            pltpu.VMEM((COLS, 16, 128), BF16),
            pltpu.VMEM((GROUPS, 256, 128 * GTILES), BF16),
            pltpu.VMEM((GROUPS, 256, 128 * GTILES), BF16),
            pltpu.VMEM((256, 128 * GTILES), BF16),
            pltpu.VMEM((256, 256), F32),
            pltpu.VMEM((16, 16, 256), BF16),
            pltpu.VMEM((16, 16, 256), BF16),
            pltpu.VMEM((32, 16, 256), BF16),
            pltpu.VMEM((RSH, SEG), BF16),
            pltpu.VMEM((16, SEG, RSH), BF16),
            pltpu.VMEM((16, CSH, SEG), BF16),
            dma((2,)),
            dma((2,)),
            dma((COLS,)),
            dma((COLS,)),
            dma((16,)),
            dma((16,)),
            dma((COLS,)),
            dma((COLS,)),
            dma((40,)),
            dma((COLS,)),
            dma((20,)),
            dma((ROWS,)),
            dma,
        ],
        compiler_params=pltpu.CompilerParams(
            collective_id=0, has_side_effects=True, vmem_limit_bytes=48 * 1024 * 1024
        ),
    )(
        design.T,
        nuisance_vals,
        arc_index.reshape(1, SEG),
        filter_taps.reshape(1, SEG),
        slots,
        normal_prior.T,
    )
    return result.T


def solution(mesh):
    return jax.shard_map(
        per_device,
        mesh=mesh,
        in_specs=(P("row", "col"), P(None, "row"), P("row"), P(), P(), P("row", "col")),
        out_specs=P("row", "col"),
        check_vma=False,
    )
```

```python
import jax
import jax.numpy as jnp
from jax import lax
from jax.experimental import pallas as pl
from jax.experimental.pallas import tpu as pltpu
from jax.sharding import PartitionSpec as P

MESH = pl.DeviceIdType.MESH
F32, BF16 = jnp.float32, jnp.bfloat16

ROWS, COLS = 16, 32
NPA, NUIS = 4, 256
SEG = 128
COEF_W = 440
TT = 4
RSH, CSH = 896, 448
GROUPS, GTILES = 16, 8


def nt(a, b):
    return lax.dot_general(a, b, (((1,), (1,)), ((), ())), preferred_element_type=F32)


def nn(a, b):
    return lax.dot_general(a, b, (((1,), (0,)), ((), ())), preferred_element_type=F32)


def iota(shape, dim):
    return lax.broadcasted_iota(jnp.int32, shape, dim)


def remote(src, dst, send_sem, recv_sem, row, col):
    return pltpu.make_async_remote_copy(
        src_ref=src,
        dst_ref=dst,
        send_sem=send_sem,
        recv_sem=recv_sem,
        device_id=(row, col),
        device_id_type=MESH,
    )


def kernel(
    design,
    vals_hbm,
    arcs_hbm,
    taps_hbm,
    ordering_hbm,
    out,
    vals,
    arcs,
    taps,
    ordering,
    slots,
    own,
    halo,
    nown,
    nhalo,
    wbuf,
    p1,
    hot_hi,
    hot_lo,
    xg,
    oacc,
    obuf,
    a2,
    b2,
    abuf,
    bbuf,
    btr,
    load_sem,
    hsend,
    hrecv,
    psend,
    precv,
    asend,
    arecv,
    bsend,
    brecv,
    gsend,
    grecv,
    qsend,
    qrecv,
):
    r, c = lax.axis_index("row"), lax.axis_index("col")
    y, zl0 = c % 8, c // 8
    xi = (r // 2) % 4
    rbase = r - 2 * xi
    r_core = r + 1 - 2 * (r % 2)
    r_z = (r + 8) % ROWS
    r_next, r_prev = (r + 1) % ROWS, (r + ROWS - 1) % ROWS

    def r_x(row, d):
        return row - 2 * xi + 2 * ((xi + d) % 4)

    loads = [
        pltpu.make_async_copy(src, dst, load_sem.at[n])
        for n, (src, dst) in enumerate(
            ((vals_hbm, vals), (arcs_hbm, arcs), (taps_hbm, taps), (ordering_hbm, ordering))
        )
    ]
    for load in loads:
        load.start()

    barrier = pltpu.get_barrier_semaphore()

    def tell(row, col):
        pl.semaphore_signal(barrier, inc=1, device_id=(row, col), device_id_type=MESH)

    @pl.loop(1, ROWS)
    def _(i):
        tell((r + i) % ROWS, c)

    @pl.loop(1, COLS)
    def _(i):
        tell(r, (c + i) % COLS)

    out[...] = jnp.zeros((CSH, RSH), F32)
    own[...] = jnp.zeros((512, SEG), BF16)
    own[0:COEF_W, :] = design[...]
    for load in loads:
        load.wait()
    nown[0:4, :] = vals[...]
    nown[4:8, :] = jnp.broadcast_to(arcs[...].astype(F32), (4, SEG))

    pl.semaphore_wait(barrier, ROWS + COLS - 2)

    halo_copies = [
        remote(own.at[pl.ds(0, 448)], halo.at[pl.ds(0, 448)], hsend.at[0], hrecv.at[0], r_next, c),
        remote(nown, nhalo, hsend.at[1], hrecv.at[1], r_next, c),
    ]
    for copy in halo_copies:
        copy.start()

    lane = iota((1, 128), 1)
    for src in range(COLS):
        for q in range(4):
            first = COEF_W * src + 128 * q
            tile, off = first // 128, first % 128
            line = ordering[tile : tile + 1]
            if off:
                line = jnp.where(lane >= off, line, ordering[tile + 1 : tile + 2])
                line = pltpu.roll(line, 128 - off, 1)
            if q == 3:
                line = jnp.where(lane < COEF_W - 384, line, -1)
            slots[4 * src + q : 4 * src + q + 1] = line
    slots[128:130] = ordering[COLS * COEF_W // 128 :]

    hp = (iota((256, 128), 0) // 4).astype(F32)
    lp = iota((256, 128), 0).astype(F32)

    def factors(rows):
        s = rows.astype(F32)
        cc = jnp.floor((s + 0.5) * (1.0 / CSH))
        odd = cc - 2.0 * jnp.floor(cc * 0.5)
        u = s - cc * CSH + 64.0 * odd
        h = jnp.floor((u + 0.5) * (1.0 / 256.0))
        return jnp.where(rows < 0, -1.0, 2.0 * cc + h), u - 256.0 * h

    def one_hot(row, pattern):
        return jnp.where(jnp.broadcast_to(row, pattern.shape) == pattern, 1.0, 0.0).astype(BF16)

    @pl.loop(0, GROUPS)
    def _(g):
        hi, lo = factors(slots[pl.ds(pl.multiple_of(8 * g, 8), 8), :])
        for i in range(GTILES):
            hot_hi[g, :, 128 * i : 128 * i + 128] = one_hot(hi[i : i + 1], hp)
            hot_lo[g, :, 128 * i : 128 * i + 128] = one_hot(lo[i : i + 1], lp)

    line = jnp.concatenate([taps[...], jnp.zeros((1, SEG), F32)], 1)
    band = pltpu.roll(jnp.broadcast_to(line, (SEG, 2 * SEG)), 0, 1, stride=1, stride_axis=0)
    has_past = jnp.where(r > 0, 1.0, 0.0).astype(F32)
    band_now, band_past = band[:, :SEG], band[:, SEG:] * has_past

    def split(x):
        high = x.astype(BF16)
        return high, (x - high.astype(F32)).astype(BF16)

    now_hi, now_lo = split(band_now)
    past_hi, past_lo = split(band_past)

    for copy in halo_copies:
        copy.wait()

    mine = own[...]
    past = halo[0:448, :]
    filtered = nn(mine, now_hi) + nn(mine, now_lo)
    part = nn(past, past_hi) + nn(past, past_lo)
    filtered = jnp.concatenate([filtered[0:448] + part, filtered[448:512]], 0).astype(BF16)
    p_row, p_time = iota((512, 128), 0), iota((512, 128), 1)
    at_time = p_time == TT * (p_row // 16) + p_row % 4
    wsum = jnp.zeros((512, 128), F32)
    for q in range(4):
        pick = jnp.where(at_time & ((p_row // 4) % 4 == q), 1.0, 0.0).astype(BF16)
        wsum = wsum + nt(pick, filtered[128 * q : 128 * q + 128])
    wbuf[...] = wsum.astype(BF16).reshape(COLS, 16, 128)

    p1[c] = wbuf[c]

    @pl.loop(1, COLS)
    def _(i):
        to = (c + i) % COLS
        remote(wbuf.at[to], p1.at[c], psend.at[i], precv.at[c], r, to).start()

    n_row = iota((NUIS, SEG), 0)

    def nuisance(ref):
        v = jnp.broadcast_to(ref[0:1], (NUIS, SEG))
        for q in range(1, NPA):
            v = jnp.where(n_row % NPA == q, jnp.broadcast_to(ref[q : q + 1], (NUIS, SEG)), v)
        arc = jnp.broadcast_to(ref[4:5], (NUIS, SEG))
        return jnp.where(arc == (n_row // NPA).astype(F32), v, 0.0)

    def exact(a, b):
        return lax.dot_general(
            a, b, (((1,), (0,)), ((), ())), precision=lax.Precision.HIGHEST, preferred_element_type=F32
        )

    nfil = (exact(nuisance(nown), band_now) + exact(nuisance(nhalo), band_past)).astype(BF16)
    s_row, s_time = iota((16, 128), 0), iota((16, 128), 1)
    pick = jnp.where(s_time == TT * c + s_row % 4, 1.0, 0.0).astype(BF16)
    nhi, nlo = factors(slots[128:130, :])
    accum = jnp.zeros((256, 256), F32)
    for q in range(2):
        rep = nt(pick, nfil[128 * q : 128 * q + 128]).astype(BF16)
        x = jnp.concatenate([rep] * 16, 0) * one_hot(nhi[q : q + 1], hp)
        accum = accum + nt(x, one_hot(nlo[q : q + 1], lp))
    oacc[...] = accum

    @pl.loop(1, COLS)
    def _(i):
        src = (c + COLS - i) % COLS
        remote(wbuf.at[src], p1.at[src], psend.at[i], precv.at[src], r, src).wait()

    low4 = iota((8, 128), 0) < 4

    @pl.loop(0, GROUPS)
    def _(g):
        for k in range(2):
            msg = p1[2 * g + k].astype(F32)
            for v in range(2):
                part = msg[8 * v : 8 * v + 8]
                rot = pltpu.roll(part, 4, 0)
                for u in range(2):
                    rep = jnp.where(low4, part, rot) if u == 0 else jnp.where(low4, rot, part)
                    rep = jnp.concatenate([rep, rep], 0).astype(BF16)
                    i = 4 * k + 2 * v + u
                    lanes = slice(128 * i, 128 * i + 128)
                    xg[:, lanes] = jnp.concatenate([rep] * 16, 0) * hot_hi[g, :, lanes]
        oacc[...] += nt(xg[...], hot_lo[g])

    for cc in range(COLS):
        block = oacc[8 * cc : 8 * cc + 8]
        obuf[cc] = jnp.concatenate([block[:, :128], block[:, 128:]], 0).astype(BF16)

    @pl.loop(1, ROWS)
    def _(i):
        to = (r + i) % ROWS
        remote(obuf.at[pl.ds(2 * to, 2)], a2.at[r], asend.at[i], arecv.at[r], to, c).start()

    @pl.loop(1, COLS)
    def _(i):
        to = (c + i) % COLS
        remote(obuf.at[to], b2.at[c], bsend.at[i], brecv.at[c], r, to).start()

    a2[r] = obuf[pl.ds(2 * r, 2)]
    b2[c] = obuf[c]

    m, p = iota((448, 512), 0), iota((448, 512), 1)
    tile = 3 * ((p // 16) % 2) + 2 * ((p // 4) % 2) + (p // 8) % 2
    same = (p // 32 == (m % 64) // 4) & (p % 4 == m % 4)
    pick = jnp.where(same & (tile == m // 64), 1.0, 0.0).astype(BF16)

    @pl.loop(1, ROWS)
    def _(i):
        src = (r + ROWS - i) % ROWS
        remote(a2.at[src], a2.at[src], asend.at[i], arecv.at[src], src, c).wait()

    pieces = nn(pick, a2[...].reshape(512, 128)).astype(BF16)
    for j in range(7):
        abuf[c, :, 128 * j : 128 * j + 128] = pieces[64 * j : 64 * j + 64]

    def chunk(zl, yy):
        return abuf.at[zl * 8 + yy]

    y_of = [(y + d) % 8 for d in range(8)]
    zls = [(zl0 + k) % 4 for k in range(4)]
    sends = []

    def pass_on(k, dist, direction):
        yy = y_of[(-direction * dist) % 8]
        n = len(sends)
        copy = remote(
            chunk(zls[k], yy),
            chunk(zls[k], yy),
            gsend.at[n],
            grecv.at[zls[k] * 8 + yy],
            r,
            zl0 * 8 + y_of[direction % 8],
        )
        copy.start()
        sends.append(copy)

    def arrived(zl, yy):
        remote(chunk(zl, yy), chunk(zl, yy), gsend.at[0], grecv.at[zl * 8 + yy], r, c).wait_recv()

    pass_on(0, 0, 1)
    pass_on(0, 0, -1)
    for k in (1, 3, 2):
        copy = remote(
            chunk(zl0, y), chunk(zl0, y), gsend.at[len(sends)], grecv.at[c], r, zls[k] * 8 + y
        )
        copy.start()
        sends.append(copy)

    m, p = iota((512, 512), 0), iota((512, 512), 1)
    tile = 2 * ((p // 4) % 2) + (p // 8) % 2
    same = (p // 16 == (m % 128) // 4) & (p % 4 == m % 4)
    pick = jnp.where(same & (tile == m // 128), 1.0, 0.0).astype(BF16)

    @pl.loop(1, COLS)
    def _(i):
        src = (c + COLS - i) % COLS
        remote(b2.at[src], b2.at[src], bsend.at[i], brecv.at[src], r, src).wait()

    pieces = nn(pick, b2[...].reshape(512, 128)).astype(BF16)
    for j in range(4):
        bbuf[r, :, 128 * j : 128 * j + 128] = pieces[128 * j : 128 * j + 128]

    bsends = []

    def spread(row, to):
        n = len(bsends)
        copy = remote(bbuf.at[row], bbuf.at[row], qsend.at[n], qrecv.at[row], to, c)
        copy.start()
        bsends.append(copy)

    def b_arrived(row):
        remote(bbuf.at[row], bbuf.at[row], qsend.at[0], qrecv.at[row], r, c).wait_recv()

    spread(r, r_z)
    for d in (1, 3, 2):
        spread(r, r_x(r, d))
    spread(r, r_core)

    for k in (1, 3, 2):
        arrived(zls[k], y)
        pass_on(k, 0, 1)
        pass_on(k, 0, -1)

    b_arrived(r_z)
    for d in (1, 3, 2):
        spread(r_z, r_x(r, d))
    spread(r_z, r_core)

    def product(k, y_half):
        quad = zls[k] * 2 + y_half
        b = btr[quad, pl.ds(pl.multiple_of(64 * (c % 2), 64), CSH), :]
        out[...] += nn(b, abuf[pl.ds(4 * quad, 4)].reshape(256, RSH))

    for s in range(1, 5):
        for k in range(4):
            right, left = (4, 3) if k % 2 == 0 else (3, 4)
            if s <= right:
                arrived(zls[k], y_of[-s % 8])
                if s < right:
                    pass_on(k, s, 1)
            if s <= left:
                arrived(zls[k], y_of[s % 8])
                if s < left:
                    pass_on(k, s, -1)
            if s == 3:
                product(k, y // 4)
            if s == 4:
                product(k, 1 - y // 4)
        if s == 1:
            for base in (r, r_z):
                for d in (1, 3, 2):
                    b_arrived(r_x(base, d))
                    spread(r_x(base, d), r_core)
        if s == 2:
            for base in (r, r_z):
                for d in range(4):
                    row = r_x(base, d)
                    b_arrived(row + 1 - 2 * (row % 2))
            m, p = iota((256, 256), 0), iota((256, 256), 1)
            same = (p // 16 == (m // 4) % 16) & (p % 4 == m % 4) & ((p // 4) % 4 == m // 64)
            pick = jnp.where(same, 1.0, 0.0).astype(BF16)

            @pl.loop(0, 8)
            def _(n):
                rows = bbuf[:, pl.ds(pl.multiple_of(16 * n, 16), 16), :].reshape(256, 512)
                btr[n] = nn(pick, rows).T.astype(BF16)

    for copy in sends + bsends:
        copy.wait_send()


def per_device(design, nuisance_vals, arc_index, filter_taps, ordering, normal_prior):
    vmem = pl.BlockSpec(memory_space=pltpu.VMEM)
    dma = pltpu.SemaphoreType.DMA
    result = pl.pallas_call(
        kernel,
        out_shape=jax.ShapeDtypeStruct((CSH, RSH), F32),
        in_specs=[vmem] + [pl.BlockSpec(memory_space=pltpu.HBM)] * 4,
        out_specs=vmem,
        scratch_shapes=[
            pltpu.VMEM((NPA, SEG), F32),
            pltpu.VMEM((1, SEG), jnp.int32),
            pltpu.VMEM((1, SEG), F32),
            pltpu.VMEM((112, 128), jnp.int32),
            pltpu.VMEM((136, 128), jnp.int32),
            pltpu.VMEM((512, SEG), BF16),
            pltpu.VMEM((512, SEG), BF16),
            pltpu.VMEM((8, SEG), F32),
            pltpu.VMEM((8, SEG), F32),
            pltpu.VMEM((COLS, 16, 128), BF16),
            pltpu.VMEM((COLS, 16, 128), BF16),
            pltpu.VMEM((GROUPS, 256, 128 * GTILES), BF16),
            pltpu.VMEM((GROUPS, 256, 128 * GTILES), BF16),
            pltpu.VMEM((256, 128 * GTILES), BF16),
            pltpu.VMEM((256, 256), F32),
            pltpu.VMEM((COLS, 16, 128), BF16),
            pltpu.VMEM((ROWS, 2, 16, 128), BF16),
            pltpu.VMEM((COLS, 16, 128), BF16),
            pltpu.VMEM((COLS, 64, RSH), BF16),
            pltpu.VMEM((ROWS, SEG, 512), BF16),
            pltpu.VMEM((8, 512, 256), BF16),
            dma((4,)),
            dma((2,)),
            dma((2,)),
            dma((COLS,)),
            dma((COLS,)),
            dma((16,)),
            dma((16,)),
            dma((COLS,)),
            dma((COLS,)),
            dma((40,)),
            dma((COLS,)),
            dma((20,)),
            dma((ROWS,)),
        ],
        compiler_params=pltpu.CompilerParams(
            collective_id=0, has_side_effects=True, vmem_limit_bytes=48 * 1024 * 1024
        ),
    )(
        design.T,
        nuisance_vals,
        arc_index.reshape(1, SEG),
        filter_taps.reshape(1, SEG),
        ordering.reshape(112, 128),
    )
    return normal_prior + result.T


def solution(mesh):
    return jax.shard_map(
        per_device,
        mesh=mesh,
        in_specs=(P("row", "col"), P(None, "row"), P("row"), P(), P(), P("row", "col")),
        out_specs=P("row", "col"),
        check_vma=False,
    )
```

```python
import jax
import jax.numpy as jnp
from jax import lax
from jax.experimental import pallas as pl
from jax.experimental.pallas import tpu as pltpu
from jax.sharding import PartitionSpec as P

MESH = pl.DeviceIdType.MESH
F32, BF16 = jnp.float32, jnp.bfloat16

ROWS, COLS = 16, 32
NPA, NUIS = 4, 256
SEG = 128
COEF_W = 440
TT = 4
RSH, CSH = 896, 448
GROUPS, GTILES = 16, 8


def nt(a, b):
    return lax.dot_general(a, b, (((1,), (1,)), ((), ())), preferred_element_type=F32)


def nn(a, b):
    return lax.dot_general(a, b, (((1,), (0,)), ((), ())), preferred_element_type=F32)


def iota(shape, dim):
    return lax.broadcasted_iota(jnp.int32, shape, dim)


def remote(src, dst, send_sem, recv_sem, row, col):
    return pltpu.make_async_remote_copy(
        src_ref=src,
        dst_ref=dst,
        send_sem=send_sem,
        recv_sem=recv_sem,
        device_id=(row, col),
        device_id_type=MESH,
    )


def kernel(
    design,
    vals_hbm,
    arcs_hbm,
    taps_hbm,
    ordering_hbm,
    prior_hbm,
    out,
    vals,
    arcs,
    taps,
    ordering,
    slots,
    own,
    halo,
    nown,
    nhalo,
    wbuf,
    p1,
    hot_hi,
    hot_lo,
    xg,
    oacc,
    obuf,
    a2,
    b2,
    pbuf,
    qbuf,
    bbuf,
    btr,
    load_sem,
    prior_sem,
    hsend,
    hrecv,
    psend,
    precv,
    asend,
    arecv,
    bsend,
    brecv,
    gsend,
    grecv,
    ssend,
    srecv,
    lsend,
    lrecv,
    qsend,
    qrecv,
):
    r, c = lax.axis_index("row"), lax.axis_index("col")
    y, zl0 = c % 8, c // 8
    xi = (r // 2) % 4
    rbase = r - 2 * xi
    r_core = r + 1 - 2 * (r % 2)
    r_z = (r + 8) % ROWS
    r_next, r_prev = (r + 1) % ROWS, (r + ROWS - 1) % ROWS

    def r_x(row, d):
        return row - 2 * xi + 2 * ((xi + d) % 4)

    loads = [
        pltpu.make_async_copy(src, dst, load_sem.at[n])
        for n, (src, dst) in enumerate(
            ((vals_hbm, vals), (arcs_hbm, arcs), (taps_hbm, taps), (ordering_hbm, ordering))
        )
    ]
    for load in loads:
        load.start()
    prior_load = pltpu.make_async_copy(prior_hbm, out, prior_sem)
    prior_load.start()

    barrier = pltpu.get_barrier_semaphore()

    def tell(row, col):
        pl.semaphore_signal(barrier, inc=1, device_id=(row, col), device_id_type=MESH)

    @pl.loop(1, ROWS)
    def _(i):
        tell((r + i) % ROWS, c)

    @pl.loop(1, COLS)
    def _(i):
        tell(r, (c + i) % COLS)

    own[...] = jnp.zeros((512, SEG), BF16)
    own[0:COEF_W, :] = design[...]
    for load in loads:
        load.wait()
    nown[0:4, :] = vals[...]
    nown[4:8, :] = jnp.broadcast_to(arcs[...].astype(F32), (4, SEG))

    pl.semaphore_wait(barrier, ROWS + COLS - 2)

    halo_copies = [
        remote(own.at[pl.ds(0, 448)], halo.at[pl.ds(0, 448)], hsend.at[0], hrecv.at[0], r_next, c),
        remote(nown, nhalo, hsend.at[1], hrecv.at[1], r_next, c),
    ]
    for copy in halo_copies:
        copy.start()

    lane = iota((1, 128), 1)
    for src in range(COLS):
        for q in range(4):
            first = COEF_W * src + 128 * q
            tile, off = first // 128, first % 128
            line = ordering[tile : tile + 1]
            if off:
                line = jnp.where(lane >= off, line, ordering[tile + 1 : tile + 2])
                line = pltpu.roll(line, 128 - off, 1)
            if q == 3:
                line = jnp.where(lane < COEF_W - 384, line, -1)
            slots[4 * src + q : 4 * src + q + 1] = line
    slots[128:130] = ordering[COLS * COEF_W // 128 :]

    hp = (iota((256, 128), 0) // 4).astype(F32)
    lp = iota((256, 128), 0).astype(F32)

    def factors(rows):
        s = rows.astype(F32)
        cc = jnp.floor((s + 0.5) * (1.0 / CSH))
        odd = cc - 2.0 * jnp.floor(cc * 0.5)
        u = s - cc * CSH + 64.0 * odd
        h = jnp.floor((u + 0.5) * (1.0 / 256.0))
        return jnp.where(rows < 0, -1.0, 2.0 * cc + h), u - 256.0 * h

    def one_hot(row, pattern):
        return jnp.where(jnp.broadcast_to(row, pattern.shape) == pattern, 1.0, 0.0).astype(BF16)

    @pl.loop(0, GROUPS)
    def _(g):
        hi, lo = factors(slots[pl.ds(pl.multiple_of(8 * g, 8), 8), :])
        for i in range(GTILES):
            hot_hi[g, :, 128 * i : 128 * i + 128] = one_hot(hi[i : i + 1], hp)
            hot_lo[g, :, 128 * i : 128 * i + 128] = one_hot(lo[i : i + 1], lp)

    line = jnp.concatenate([taps[...], jnp.zeros((1, SEG), F32)], 1)
    band = pltpu.roll(jnp.broadcast_to(line, (SEG, 2 * SEG)), 0, 1, stride=1, stride_axis=0)
    has_past = jnp.where(r > 0, 1.0, 0.0).astype(F32)
    band_now, band_past = band[:, :SEG], band[:, SEG:] * has_past

    def split(x):
        high = x.astype(BF16)
        return high, (x - high.astype(F32)).astype(BF16)

    now_hi, now_lo = split(band_now)
    past_hi, past_lo = split(band_past)

    for copy in halo_copies:
        copy.wait()

    mine = own[...]
    past = halo[0:448, :]
    filtered = nn(mine, now_hi) + nn(mine, now_lo)
    part = nn(past, past_hi) + nn(past, past_lo)
    filtered = jnp.concatenate([filtered[0:448] + part, filtered[448:512]], 0).astype(BF16)
    p_row, p_time = iota((512, 128), 0), iota((512, 128), 1)
    at_time = p_time == TT * (p_row // 16) + p_row % 4
    wsum = jnp.zeros((512, 128), F32)
    for q in range(4):
        pick = jnp.where(at_time & ((p_row // 4) % 4 == q), 1.0, 0.0).astype(BF16)
        wsum = wsum + nt(pick, filtered[128 * q : 128 * q + 128])
    wbuf[...] = wsum.astype(BF16).reshape(COLS, 16, 128)

    p1[c] = wbuf[c]

    @pl.loop(1, COLS)
    def _(i):
        to = (c + i) % COLS
        remote(wbuf.at[to], p1.at[c], psend.at[i], precv.at[c], r, to).start()

    n_row = iota((NUIS, SEG), 0)

    def nuisance(ref):
        v = jnp.broadcast_to(ref[0:1], (NUIS, SEG))
        for q in range(1, NPA):
            v = jnp.where(n_row % NPA == q, jnp.broadcast_to(ref[q : q + 1], (NUIS, SEG)), v)
        arc = jnp.broadcast_to(ref[4:5], (NUIS, SEG))
        return jnp.where(arc == (n_row // NPA).astype(F32), v, 0.0)

    def exact(a, b):
        return lax.dot_general(
            a, b, (((1,), (0,)), ((), ())), precision=lax.Precision.HIGHEST, preferred_element_type=F32
        )

    nfil = (exact(nuisance(nown), band_now) + exact(nuisance(nhalo), band_past)).astype(BF16)
    s_row, s_time = iota((16, 128), 0), iota((16, 128), 1)
    pick = jnp.where(s_time == TT * c + s_row % 4, 1.0, 0.0).astype(BF16)
    nhi, nlo = factors(slots[128:130, :])
    accum = jnp.zeros((256, 256), F32)
    for q in range(2):
        rep = nt(pick, nfil[128 * q : 128 * q + 128]).astype(BF16)
        x = jnp.concatenate([rep] * 16, 0) * one_hot(nhi[q : q + 1], hp)
        accum = accum + nt(x, one_hot(nlo[q : q + 1], lp))
    oacc[...] = accum

    @pl.loop(1, COLS)
    def _(i):
        src = (c + COLS - i) % COLS
        remote(wbuf.at[src], p1.at[src], psend.at[i], precv.at[src], r, src).wait()

    low4 = iota((8, 128), 0) < 4

    @pl.loop(0, GROUPS)
    def _(g):
        for k in range(2):
            msg = p1[2 * g + k].astype(F32)
            for v in range(2):
                part = msg[8 * v : 8 * v + 8]
                rot = pltpu.roll(part, 4, 0)
                for u in range(2):
                    rep = jnp.where(low4, part, rot) if u == 0 else jnp.where(low4, rot, part)
                    rep = jnp.concatenate([rep, rep], 0).astype(BF16)
                    i = 4 * k + 2 * v + u
                    lanes = slice(128 * i, 128 * i + 128)
                    xg[:, lanes] = jnp.concatenate([rep] * 16, 0) * hot_hi[g, :, lanes]
        oacc[...] += nt(xg[...], hot_lo[g])

    for cc in range(COLS):
        block = oacc[8 * cc : 8 * cc + 8]
        obuf[cc] = jnp.concatenate([block[:, :128], block[:, 128:]], 0).astype(BF16)

    @pl.loop(1, ROWS)
    def _(i):
        to = (r + i) % ROWS
        remote(obuf.at[pl.ds(2 * to, 2)], a2.at[r], asend.at[i], arecv.at[r], to, c).start()

    @pl.loop(1, COLS)
    def _(i):
        to = (c + i) % COLS
        remote(obuf.at[to], b2.at[c], bsend.at[i], brecv.at[c], r, to).start()

    a2[r] = obuf[pl.ds(2 * r, 2)]
    b2[c] = obuf[c]

    m, p = iota((448, 512), 0), iota((448, 512), 1)
    tile = 3 * ((p // 16) % 2) + 2 * ((p // 4) % 2) + (p // 8) % 2
    same = (p // 32 == (m % 64) // 4) & (p % 4 == m % 4)
    pick = jnp.where(same & (tile == m // 64), 1.0, 0.0).astype(BF16)

    @pl.loop(1, ROWS)
    def _(i):
        src = (r + ROWS - i) % ROWS
        remote(a2.at[src], a2.at[src], asend.at[i], arecv.at[src], src, c).wait()

    pieces = nn(pick, a2[...].reshape(512, 128)).astype(BF16)
    for j in range(6):
        pbuf[c, :, 128 * j : 128 * j + 128] = pieces[64 * j : 64 * j + 64]
    qbuf[c] = pieces[384:448]

    def chunk(zl, yy):
        return pbuf.at[zl * 8 + yy]

    y_of = [(y + d) % 8 for d in range(8)]
    zls = [(zl0 + k) % 4 for k in range(4)]
    sends = []

    def pass_on(k, dist, direction):
        yy = y_of[(-direction * dist) % 8]
        n = len(sends)
        copy = remote(
            chunk(zls[k], yy),
            chunk(zls[k], yy),
            gsend.at[n],
            grecv.at[zls[k] * 8 + yy],
            r,
            zl0 * 8 + y_of[direction % 8],
        )
        copy.start()
        sends.append(copy)

    def arrived(zl, yy):
        remote(chunk(zl, yy), chunk(zl, yy), gsend.at[0], grecv.at[zl * 8 + yy], r, c).wait_recv()

    qsends = []

    def q_pass(dist, direction):
        piece = qbuf.at[zl0 * 8 + y_of[(-direction * dist) % 8]]
        copy = remote(
            piece,
            piece,
            ssend.at[len(qsends)],
            srecv.at[y_of[(-direction * dist) % 8]],
            r,
            zl0 * 8 + y_of[direction % 8],
        )
        copy.start()
        qsends.append(copy)

    def q_arrived(yy):
        piece = qbuf.at[zl0 * 8 + yy]
        remote(piece, piece, ssend.at[0], srecv.at[yy], r, c).wait_recv()

    def q_step(s):
        q_arrived(y_of[-s % 8])
        if s < 4:
            q_pass(s, 1)
            q_arrived(y_of[s])
            if s < 3:
                q_pass(s, -1)

    def level_copy(dist, up):
        level = zl0 - dist if up else zl0 + dist
        levels = qbuf.at[pl.ds(8 * level, 8)]
        to = c + 8 if up else c - 8
        return remote(levels, levels, lsend.at[2 * dist + int(up)], lrecv.at[level], r, to)

    def level_goes(dist, up):
        return (zl0 >= dist) & (zl0 < 3) if up else (zl0 <= 3 - dist) & (zl0 > 0)

    def level_step(dist):
        for up in (True, False):
            if dist:
                level = zl0 - dist if up else zl0 + dist

                @pl.when(zl0 >= dist if up else zl0 <= 3 - dist)
                def _():
                    levels = qbuf.at[pl.ds(8 * level, 8)]
                    remote(levels, levels, lsend.at[0], lrecv.at[level], r, c).wait_recv()

            if dist < 3:

                @pl.when(level_goes(dist, up))
                def _():
                    level_copy(dist, up).start()

    q_pass(0, 1)
    q_pass(0, -1)
    pass_on(0, 0, 1)
    pass_on(0, 0, -1)
    for k in (1, 3, 2):
        copy = remote(
            chunk(zl0, y), chunk(zl0, y), gsend.at[len(sends)], grecv.at[c], r, zls[k] * 8 + y
        )
        copy.start()
        sends.append(copy)

    m, p = iota((512, 512), 0), iota((512, 512), 1)
    tile = 2 * ((p // 4) % 2) + (p // 8) % 2
    same = (p // 16 == (m % 128) // 4) & (p % 4 == m % 4)
    pick = jnp.where(same & (tile == m // 128), 1.0, 0.0).astype(BF16)

    @pl.loop(1, COLS)
    def _(i):
        src = (c + COLS - i) % COLS
        remote(b2.at[src], b2.at[src], bsend.at[i], brecv.at[src], r, src).wait()

    pieces = nn(pick, b2[...].reshape(512, 128)).astype(BF16)
    for j in range(4):
        bbuf[r, :, 128 * j : 128 * j + 128] = pieces[128 * j : 128 * j + 128]

    bsends = []

    def spread(row, to):
        n = len(bsends)
        copy = remote(bbuf.at[row], bbuf.at[row], qsend.at[n], qrecv.at[row], to, c)
        copy.start()
        bsends.append(copy)

    def b_arrived(row):
        remote(bbuf.at[row], bbuf.at[row], qsend.at[0], qrecv.at[row], r, c).wait_recv()

    spread(r, r_z)
    for d in (1, 3, 2):
        spread(r, r_x(r, d))
    spread(r, r_core)

    for n, k in enumerate((1, 3, 2)):
        q_step(n + 1)
        arrived(zls[k], y)
        pass_on(k, 0, 1)
        pass_on(k, 0, -1)
    q_step(4)
    level_step(0)

    def product(k, y_half):
        quad = zls[k] * 2 + y_half
        b = btr[quad, pl.ds(pl.multiple_of(64 * (c % 2), 64), CSH), :]
        out[:, :768] += nn(b, pbuf[pl.ds(4 * quad, 4)].reshape(256, 768))
        out[:, 768:] += nn(b, qbuf[pl.ds(4 * quad, 4)].reshape(256, 128))

    for s in range(1, 5):
        for k in range(4):
            right, left = (4, 3) if k % 2 == 0 else (3, 4)
            if s <= right:
                arrived(zls[k], y_of[-s % 8])
                if s < right:
                    pass_on(k, s, 1)
            if s <= left:
                arrived(zls[k], y_of[s % 8])
                if s < left:
                    pass_on(k, s, -1)
            if s == 4:
                product(k, 1 - y // 4)
        if s < 4:
            level_step(s)
        if s == 1:
            for d in (1, 3, 2):
                b_arrived(r_x(r, d))
                spread(r_x(r, d), r_core)
            b_arrived(r_z)
            for d in (1, 3, 2):
                spread(r_z, r_x(r, d))
            spread(r_z, r_core)
        if s == 2:
            for d in (1, 3, 2):
                b_arrived(r_x(r_z, d))
                spread(r_x(r_z, d), r_core)
        if s == 3:
            for base in (r, r_z):
                for d in range(4):
                    row = r_x(base, d)
                    b_arrived(row + 1 - 2 * (row % 2))
            m, p = iota((256, 256), 0), iota((256, 256), 1)
            same = (p // 16 == (m // 4) % 16) & (p % 4 == m % 4) & ((p // 4) % 4 == m // 64)
            pick = jnp.where(same, 1.0, 0.0).astype(BF16)

            @pl.loop(0, 8)
            def _(n):
                rows = bbuf[:, pl.ds(pl.multiple_of(16 * n, 16), 16), :].reshape(256, 512)
                btr[n] = nn(pick, rows).T.astype(BF16)

            prior_load.wait()
            for k in range(4):
                product(k, y // 4)

    for copy in sends + bsends + qsends:
        copy.wait_send()
    for dist in range(3):
        for up in (True, False):

            @pl.when(level_goes(dist, up))
            def _():
                level_copy(dist, up).wait_send()


def per_device(design, nuisance_vals, arc_index, filter_taps, ordering, normal_prior):
    vmem = pl.BlockSpec(memory_space=pltpu.VMEM)
    dma = pltpu.SemaphoreType.DMA
    result = pl.pallas_call(
        kernel,
        out_shape=jax.ShapeDtypeStruct((CSH, RSH), F32),
        in_specs=[vmem] + [pl.BlockSpec(memory_space=pl.ANY)] * 5,
        out_specs=vmem,
        scratch_shapes=[
            pltpu.VMEM((NPA, SEG), F32),
            pltpu.VMEM((1, SEG), jnp.int32),
            pltpu.VMEM((1, SEG), F32),
            pltpu.VMEM((112, 128), jnp.int32),
            pltpu.VMEM((136, 128), jnp.int32),
            pltpu.VMEM((512, SEG), BF16),
            pltpu.VMEM((512, SEG), BF16),
            pltpu.VMEM((8, SEG), F32),
            pltpu.VMEM((8, SEG), F32),
            pltpu.VMEM((COLS, 16, 128), BF16),
            pltpu.VMEM((COLS, 16, 128), BF16),
            pltpu.VMEM((GROUPS, 256, 128 * GTILES), BF16),
            pltpu.VMEM((GROUPS, 256, 128 * GTILES), BF16),
            pltpu.VMEM((256, 128 * GTILES), BF16),
            pltpu.VMEM((256, 256), F32),
            pltpu.VMEM((COLS, 16, 128), BF16),
            pltpu.VMEM((ROWS, 2, 16, 128), BF16),
            pltpu.VMEM((COLS, 16, 128), BF16),
            pltpu.VMEM((COLS, 64, 768), BF16),
            pltpu.VMEM((COLS, 64, 128), BF16),
            pltpu.VMEM((ROWS, SEG, 512), BF16),
            pltpu.VMEM((8, 512, 256), BF16),
            dma((4,)),
            dma,
            dma((2,)),
            dma((2,)),
            dma((COLS,)),
            dma((COLS,)),
            dma((16,)),
            dma((16,)),
            dma((COLS,)),
            dma((COLS,)),
            dma((40,)),
            dma((COLS,)),
            dma((8,)),
            dma((8,)),
            dma((6,)),
            dma((4,)),
            dma((20,)),
            dma((ROWS,)),
        ],
        compiler_params=pltpu.CompilerParams(
            collective_id=0, has_side_effects=True, vmem_limit_bytes=60 * 1024 * 1024
        ),
    )(
        design.T,
        nuisance_vals,
        arc_index.reshape(1, SEG),
        filter_taps.reshape(1, SEG),
        ordering.reshape(112, 128),
        normal_prior.T,
    )
    return result.T


def solution(mesh):
    return jax.shard_map(
        per_device,
        mesh=mesh,
        in_specs=(P("row", "col"), P(None, "row"), P("row"), P(), P(), P("row", "col")),
        out_specs=P("row", "col"),
        check_vma=False,
    )
```

```python
import jax
import jax.numpy as jnp
from jax import lax
from jax.experimental import pallas as pl
from jax.experimental.pallas import tpu as pltpu
from jax.sharding import PartitionSpec as P

MESH = pl.DeviceIdType.MESH
F32, BF16 = jnp.float32, jnp.bfloat16

ROWS, COLS = 16, 32
NPA, NUIS = 4, 256
SEG = 128
COEF_W = 440
TT = 4
RSH, CSH = 896, 448
GROUPS, GTILES = 16, 8


def nt(a, b):
    return lax.dot_general(a, b, (((1,), (1,)), ((), ())), preferred_element_type=F32)


def nn(a, b):
    return lax.dot_general(a, b, (((1,), (0,)), ((), ())), preferred_element_type=F32)


def iota(shape, dim):
    return lax.broadcasted_iota(jnp.int32, shape, dim)


def remote(src, dst, send_sem, recv_sem, row, col):
    return pltpu.make_async_remote_copy(
        src_ref=src,
        dst_ref=dst,
        send_sem=send_sem,
        recv_sem=recv_sem,
        device_id=(row, col),
        device_id_type=MESH,
    )


def kernel(
    design,
    small,
    prior_hbm,
    out,
    slots,
    own,
    halo,
    nown,
    nhalo,
    wbuf,
    p1,
    hot_hi,
    hot_lo,
    xg,
    oacc,
    obuf,
    a2,
    b2,
    pbuf,
    qbuf,
    bbuf,
    btr,
    prior_sem,
    hsend,
    hrecv,
    psend,
    precv,
    asend,
    arecv,
    bsend,
    brecv,
    gsend,
    grecv,
    ssend,
    srecv,
    lsend,
    lrecv,
    qsend,
    qrecv,
):
    r, c = lax.axis_index("row"), lax.axis_index("col")
    y, zl0 = c % 8, c // 8
    xi = (r // 2) % 4
    rbase = r - 2 * xi
    r_core = r + 1 - 2 * (r % 2)
    r_z = (r + 8) % ROWS
    r_next, r_prev = (r + 1) % ROWS, (r + ROWS - 1) % ROWS

    def r_x(row, d):
        return row - 2 * xi + 2 * ((xi + d) % 4)

    ordering = small[0:112]
    prior_load = pltpu.make_async_copy(prior_hbm, out, prior_sem)
    prior_load.start()

    barrier = pltpu.get_barrier_semaphore()

    def tell(row, col):
        pl.semaphore_signal(barrier, inc=1, device_id=(row, col), device_id_type=MESH)

    @pl.loop(1, ROWS)
    def _(i):
        tell((r + i) % ROWS, c)

    @pl.loop(1, COLS)
    def _(i):
        tell(r, (c + i) % COLS)

    own[...] = jnp.zeros((512, SEG), BF16)
    own[0:COEF_W, :] = design[...]
    nown[0:4, :] = small[112:116]
    nown[4:8, :] = jnp.broadcast_to(small[116:117], (4, SEG))

    pl.semaphore_wait(barrier, ROWS + COLS - 2)

    halo_copies = [
        remote(own.at[pl.ds(0, 448)], halo.at[pl.ds(0, 448)], hsend.at[0], hrecv.at[0], r_next, c),
        remote(nown, nhalo, hsend.at[1], hrecv.at[1], r_next, c),
    ]
    for copy in halo_copies:
        copy.start()

    lane = iota((1, 128), 1)
    for src in range(COLS):
        for q in range(4):
            first = COEF_W * src + 128 * q
            tile, off = first // 128, first % 128
            line = ordering[tile : tile + 1]
            if off:
                line = jnp.where(lane >= off, line, ordering[tile + 1 : tile + 2])
                line = pltpu.roll(line, 128 - off, 1)
            if q == 3:
                line = jnp.where(lane < COEF_W - 384, line, -1.0)
            slots[4 * src + q : 4 * src + q + 1] = line
    slots[128:130] = ordering[COLS * COEF_W // 128 :]

    hp = (iota((256, 128), 0) // 4).astype(F32)
    lp = iota((256, 128), 0).astype(F32)

    def factors(s):
        cc = jnp.floor((s + 0.5) * (1.0 / CSH))
        odd = cc - 2.0 * jnp.floor(cc * 0.5)
        u = s - cc * CSH + 64.0 * odd
        h = jnp.floor((u + 0.5) * (1.0 / 256.0))
        return jnp.where(s < 0.0, -1.0, 2.0 * cc + h), u - 256.0 * h

    def one_hot(row, pattern):
        return jnp.where(jnp.broadcast_to(row, pattern.shape) == pattern, 1.0, 0.0).astype(BF16)

    @pl.loop(0, GROUPS)
    def _(g):
        hi, lo = factors(slots[pl.ds(pl.multiple_of(8 * g, 8), 8), :])
        for i in range(GTILES):
            hot_hi[g, :, 128 * i : 128 * i + 128] = one_hot(hi[i : i + 1], hp)
            hot_lo[g, :, 128 * i : 128 * i + 128] = one_hot(lo[i : i + 1], lp)

    line = jnp.concatenate([small[117:118], jnp.zeros((1, SEG), F32)], 1)
    band = pltpu.roll(jnp.broadcast_to(line, (SEG, 2 * SEG)), 0, 1, stride=1, stride_axis=0)
    has_past = jnp.where(r > 0, 1.0, 0.0).astype(F32)
    band_now, band_past = band[:, :SEG], band[:, SEG:] * has_past

    def split(x):
        high = x.astype(BF16)
        return high, (x - high.astype(F32)).astype(BF16)

    now_hi, now_lo = split(band_now)
    past_hi, past_lo = split(band_past)

    for copy in halo_copies:
        copy.wait()

    mine = own[...]
    past = halo[0:448, :]
    filtered = nn(mine, now_hi) + nn(mine, now_lo)
    part = nn(past, past_hi) + nn(past, past_lo)
    filtered = jnp.concatenate([filtered[0:448] + part, filtered[448:512]], 0).astype(BF16)
    p_row, p_time = iota((512, 128), 0), iota((512, 128), 1)
    at_time = p_time == TT * (p_row // 16) + p_row % 4
    wsum = jnp.zeros((512, 128), F32)
    for q in range(4):
        pick = jnp.where(at_time & ((p_row // 4) % 4 == q), 1.0, 0.0).astype(BF16)
        wsum = wsum + nt(pick, filtered[128 * q : 128 * q + 128])
    wbuf[...] = wsum.astype(BF16).reshape(COLS, 16, 128)

    p1[c] = wbuf[c]

    @pl.loop(1, COLS)
    def _(i):
        to = (c + i) % COLS
        remote(wbuf.at[to], p1.at[c], psend.at[i], precv.at[c], r, to).start()

    n_row = iota((NUIS, SEG), 0)

    def nuisance(ref):
        v = jnp.broadcast_to(ref[0:1], (NUIS, SEG))
        for q in range(1, NPA):
            v = jnp.where(n_row % NPA == q, jnp.broadcast_to(ref[q : q + 1], (NUIS, SEG)), v)
        arc = jnp.broadcast_to(ref[4:5], (NUIS, SEG))
        return jnp.where(arc == (n_row // NPA).astype(F32), v, 0.0)

    def exact(a, b):
        return lax.dot_general(
            a, b, (((1,), (0,)), ((), ())), precision=lax.Precision.HIGHEST, preferred_element_type=F32
        )

    nfil = (exact(nuisance(nown), band_now) + exact(nuisance(nhalo), band_past)).astype(BF16)
    s_row, s_time = iota((16, 128), 0), iota((16, 128), 1)
    pick = jnp.where(s_time == TT * c + s_row % 4, 1.0, 0.0).astype(BF16)
    nhi, nlo = factors(slots[128:130, :])
    accum = jnp.zeros((256, 256), F32)
    for q in range(2):
        rep = nt(pick, nfil[128 * q : 128 * q + 128]).astype(BF16)
        x = jnp.concatenate([rep] * 16, 0) * one_hot(nhi[q : q + 1], hp)
        accum = accum + nt(x, one_hot(nlo[q : q + 1], lp))
    oacc[...] = accum

    @pl.loop(1, COLS)
    def _(i):
        src = (c + COLS - i) % COLS
        remote(wbuf.at[src], p1.at[src], psend.at[i], precv.at[src], r, src).wait()

    low4 = iota((8, 128), 0) < 4

    @pl.loop(0, GROUPS)
    def _(g):
        for k in range(2):
            msg = p1[2 * g + k].astype(F32)
            for v in range(2):
                part = msg[8 * v : 8 * v + 8]
                rot = pltpu.roll(part, 4, 0)
                for u in range(2):
                    rep = jnp.where(low4, part, rot) if u == 0 else jnp.where(low4, rot, part)
                    rep = jnp.concatenate([rep, rep], 0).astype(BF16)
                    i = 4 * k + 2 * v + u
                    lanes = slice(128 * i, 128 * i + 128)
                    xg[:, lanes] = jnp.concatenate([rep] * 16, 0) * hot_hi[g, :, lanes]
        oacc[...] += nt(xg[...], hot_lo[g])

    for cc in range(COLS):
        block = oacc[8 * cc : 8 * cc + 8]
        obuf[cc] = jnp.concatenate([block[:, :128], block[:, 128:]], 0).astype(BF16)

    @pl.loop(1, ROWS)
    def _(i):
        to = (r + i) % ROWS
        remote(obuf.at[pl.ds(2 * to, 2)], a2.at[r], asend.at[i], arecv.at[r], to, c).start()

    @pl.loop(1, COLS)
    def _(i):
        to = (c + i) % COLS
        remote(obuf.at[to], b2.at[c], bsend.at[i], brecv.at[c], r, to).start()

    a2[r] = obuf[pl.ds(2 * r, 2)]
    b2[c] = obuf[c]

    m, p = iota((448, 512), 0), iota((448, 512), 1)
    tile = 3 * ((p // 16) % 2) + 2 * ((p // 4) % 2) + (p // 8) % 2
    same = (p // 32 == (m % 64) // 4) & (p % 4 == m % 4)
    pick = jnp.where(same & (tile == m // 64), 1.0, 0.0).astype(BF16)

    @pl.loop(1, ROWS)
    def _(i):
        src = (r + ROWS - i) % ROWS
        remote(a2.at[src], a2.at[src], asend.at[i], arecv.at[src], src, c).wait()

    pieces = nn(pick, a2[...].reshape(512, 128)).astype(BF16)
    for j in range(6):
        pbuf[c, :, 128 * j : 128 * j + 128] = pieces[64 * j : 64 * j + 64]
    qbuf[c] = pieces[384:448]

    def chunk(zl, yy):
        return pbuf.at[zl * 8 + yy]

    y_of = [(y + d) % 8 for d in range(8)]
    zls = [(zl0 + k) % 4 for k in range(4)]
    sends = []

    def pass_on(k, dist, direction):
        yy = y_of[(-direction * dist) % 8]
        n = len(sends)
        copy = remote(
            chunk(zls[k], yy),
            chunk(zls[k], yy),
            gsend.at[n],
            grecv.at[zls[k] * 8 + yy],
            r,
            zl0 * 8 + y_of[direction % 8],
        )
        copy.start()
        sends.append(copy)

    def arrived(zl, yy):
        remote(chunk(zl, yy), chunk(zl, yy), gsend.at[0], grecv.at[zl * 8 + yy], r, c).wait_recv()

    qsends = []

    def q_pass(dist, direction):
        piece = qbuf.at[zl0 * 8 + y_of[(-direction * dist) % 8]]
        copy = remote(
            piece,
            piece,
            ssend.at[len(qsends)],
            srecv.at[y_of[(-direction * dist) % 8]],
            r,
            zl0 * 8 + y_of[direction % 8],
        )
        copy.start()
        qsends.append(copy)

    def q_arrived(yy):
        piece = qbuf.at[zl0 * 8 + yy]
        remote(piece, piece, ssend.at[0], srecv.at[yy], r, c).wait_recv()

    def q_step(s):
        q_arrived(y_of[-s % 8])
        if s < 4:
            q_pass(s, 1)
            q_arrived(y_of[s])
            if s < 3:
                q_pass(s, -1)

    def level_copy(dist, up):
        level = zl0 - dist if up else zl0 + dist
        levels = qbuf.at[pl.ds(8 * level, 8)]
        to = c + 8 if up else c - 8
        return remote(levels, levels, lsend.at[2 * dist + int(up)], lrecv.at[level], r, to)

    def level_goes(dist, up):
        return (zl0 >= dist) & (zl0 < 3) if up else (zl0 <= 3 - dist) & (zl0 > 0)

    def level_step(dist):
        for up in (True, False):
            if dist:
                level = zl0 - dist if up else zl0 + dist

                @pl.when(zl0 >= dist if up else zl0 <= 3 - dist)
                def _():
                    levels = qbuf.at[pl.ds(8 * level, 8)]
                    remote(levels, levels, lsend.at[0], lrecv.at[level], r, c).wait_recv()

            if dist < 3:

                @pl.when(level_goes(dist, up))
                def _():
                    level_copy(dist, up).start()

    q_pass(0, 1)
    q_pass(0, -1)
    pass_on(0, 0, 1)
    pass_on(0, 0, -1)
    for k in (1, 3, 2):
        copy = remote(
            chunk(zl0, y), chunk(zl0, y), gsend.at[len(sends)], grecv.at[c], r, zls[k] * 8 + y
        )
        copy.start()
        sends.append(copy)

    m, p = iota((512, 512), 0), iota((512, 512), 1)
    tile = 2 * ((p // 4) % 2) + (p // 8) % 2
    same = (p // 16 == (m % 128) // 4) & (p % 4 == m % 4)
    pick = jnp.where(same & (tile == m // 128), 1.0, 0.0).astype(BF16)

    @pl.loop(1, COLS)
    def _(i):
        src = (c + COLS - i) % COLS
        remote(b2.at[src], b2.at[src], bsend.at[i], brecv.at[src], r, src).wait()

    pieces = nn(pick, b2[...].reshape(512, 128)).astype(BF16)
    for j in range(4):
        bbuf[r, :, 128 * j : 128 * j + 128] = pieces[128 * j : 128 * j + 128]

    bsends = []

    def spread(row, to):
        n = len(bsends)
        copy = remote(bbuf.at[row], bbuf.at[row], qsend.at[n], qrecv.at[row], to, c)
        copy.start()
        bsends.append(copy)

    def b_arrived(row):
        remote(bbuf.at[row], bbuf.at[row], qsend.at[0], qrecv.at[row], r, c).wait_recv()

    for d in (1, 3, 2):
        spread(r, r_x(r, d))
    spread(r, r_core)

    for n, k in enumerate((1, 3, 2)):
        q_step(n + 1)
        arrived(zls[k], y)
        pass_on(k, 0, 1)
        pass_on(k, 0, -1)
    q_step(4)
    spread(r, r_z)
    level_step(0)

    def product(k, y_half):
        quad = zls[k] * 2 + y_half
        b = btr[quad, pl.ds(pl.multiple_of(64 * (c % 2), 64), CSH), :]
        out[:, :768] += nn(b, pbuf[pl.ds(4 * quad, 4)].reshape(256, 768))
        out[:, 768:] += nn(b, qbuf[pl.ds(4 * quad, 4)].reshape(256, 128))

    for s in range(1, 5):
        for k in range(4):
            right, left = (4, 3) if k % 2 == 0 else (3, 4)
            if s <= right:
                arrived(zls[k], y_of[-s % 8])
                if s < right:
                    pass_on(k, s, 1)
            if s <= left:
                arrived(zls[k], y_of[s % 8])
                if s < left:
                    pass_on(k, s, -1)
            if s == 4:
                product(k, 1 - y // 4)
        if s < 4:
            level_step(s)
        if s == 1:
            for d in (1, 3, 2):
                b_arrived(r_x(r, d))
                spread(r_x(r, d), r_core)
            b_arrived(r_z)
            for d in (1, 3, 2):
                spread(r_z, r_x(r, d))
            spread(r_z, r_core)
        if s == 2:
            for d in (1, 3, 2):
                b_arrived(r_x(r_z, d))
                spread(r_x(r_z, d), r_core)
        if s == 3:
            for base in (r, r_z):
                for d in range(4):
                    row = r_x(base, d)
                    b_arrived(row + 1 - 2 * (row % 2))
            m, p = iota((256, 256), 0), iota((256, 256), 1)
            same = (p // 16 == (m // 4) % 16) & (p % 4 == m % 4) & ((p // 4) % 4 == m // 64)
            pick = jnp.where(same, 1.0, 0.0).astype(BF16)

            @pl.loop(0, 8)
            def _(n):
                rows = bbuf[:, pl.ds(pl.multiple_of(16 * n, 16), 16), :].reshape(256, 512)
                btr[n] = nn(pick, rows).T.astype(BF16)

            prior_load.wait()
            for k in range(4):
                product(k, y // 4)

    for copy in sends + bsends + qsends:
        copy.wait_send()
    for dist in range(3):
        for up in (True, False):

            @pl.when(level_goes(dist, up))
            def _():
                level_copy(dist, up).wait_send()


def per_device(design, nuisance_vals, arc_index, filter_taps, ordering, normal_prior):
    vmem = pl.BlockSpec(memory_space=pltpu.VMEM)
    dma = pltpu.SemaphoreType.DMA
    small = jnp.concatenate(
        [
            ordering.astype(F32).reshape(112, SEG),
            nuisance_vals,
            arc_index.astype(F32).reshape(1, SEG),
            filter_taps.reshape(1, SEG),
            jnp.zeros((2, SEG), F32),
        ],
        0,
    )
    result = pl.pallas_call(
        kernel,
        out_shape=jax.ShapeDtypeStruct((CSH, RSH), F32),
        in_specs=[vmem, vmem, pl.BlockSpec(memory_space=pl.ANY)],
        out_specs=vmem,
        scratch_shapes=[
            pltpu.VMEM((136, 128), F32),
            pltpu.VMEM((512, SEG), BF16),
            pltpu.VMEM((512, SEG), BF16),
            pltpu.VMEM((8, SEG), F32),
            pltpu.VMEM((8, SEG), F32),
            pltpu.VMEM((COLS, 16, 128), BF16),
            pltpu.VMEM((COLS, 16, 128), BF16),
            pltpu.VMEM((GROUPS, 256, 128 * GTILES), BF16),
            pltpu.VMEM((GROUPS, 256, 128 * GTILES), BF16),
            pltpu.VMEM((256, 128 * GTILES), BF16),
            pltpu.VMEM((256, 256), F32),
            pltpu.VMEM((COLS, 16, 128), BF16),
            pltpu.VMEM((ROWS, 2, 16, 128), BF16),
            pltpu.VMEM((COLS, 16, 128), BF16),
            pltpu.VMEM((COLS, 64, 768), BF16),
            pltpu.VMEM((COLS, 64, 128), BF16),
            pltpu.VMEM((ROWS, SEG, 512), BF16),
            pltpu.VMEM((8, 512, 256), BF16),
            dma,
            dma((2,)),
            dma((2,)),
            dma((COLS,)),
            dma((COLS,)),
            dma((16,)),
            dma((16,)),
            dma((COLS,)),
            dma((COLS,)),
            dma((40,)),
            dma((COLS,)),
            dma((8,)),
            dma((8,)),
            dma((6,)),
            dma((4,)),
            dma((20,)),
            dma((ROWS,)),
        ],
        compiler_params=pltpu.CompilerParams(
            collective_id=0, has_side_effects=True, vmem_limit_bytes=52 * 1024 * 1024
        ),
    )(
        design.T,
        small,
        normal_prior.T,
    )
    return result.T


def solution(mesh):
    return jax.shard_map(
        per_device,
        mesh=mesh,
        in_specs=(P("row", "col"), P(None, "row"), P("row"), P(), P(), P("row", "col")),
        out_specs=P("row", "col"),
        check_vma=False,
    )
```

```python
import jax
import jax.numpy as jnp
from jax import lax
from jax.experimental import pallas as pl
from jax.experimental.pallas import tpu as pltpu
from jax.sharding import PartitionSpec as P

MESH = pl.DeviceIdType.MESH
F32, BF16 = jnp.float32, jnp.bfloat16

ROWS, COLS = 16, 32
NPA, NUIS = 4, 256
SEG = 128
COEF_W = 440
TT = 4
RSH, CSH = 896, 448
GROUPS, GTILES = 16, 8


def nt(a, b):
    return lax.dot_general(a, b, (((1,), (1,)), ((), ())), preferred_element_type=F32)


def nn(a, b):
    return lax.dot_general(a, b, (((1,), (0,)), ((), ())), preferred_element_type=F32)


def iota(shape, dim):
    return lax.broadcasted_iota(jnp.int32, shape, dim)


def remote(src, dst, send_sem, recv_sem, row, col):
    return pltpu.make_async_remote_copy(
        src_ref=src,
        dst_ref=dst,
        send_sem=send_sem,
        recv_sem=recv_sem,
        device_id=(row, col),
        device_id_type=MESH,
    )


def kernel(
    design,
    small,
    prior_hbm,
    out,
    slots,
    own,
    halo,
    nown,
    nhalo,
    wbuf,
    p1,
    hot_hi,
    hot_lo,
    xg,
    oacc,
    obuf,
    a2,
    b2,
    pbuf,
    qbuf,
    bbuf,
    btr,
    prior_sem,
    hsend,
    hrecv,
    psend,
    precv,
    asend,
    arecv,
    bsend,
    brecv,
    gsend,
    grecv,
    ssend,
    srecv,
    lsend,
    lrecv,
    qsend,
    qrecv,
):
    r, c = lax.axis_index("row"), lax.axis_index("col")
    y, zl0 = c % 8, c // 8
    xi = (r // 2) % 4
    rbase = r - 2 * xi
    r_core = r + 1 - 2 * (r % 2)
    r_z = (r + 8) % ROWS
    r_next, r_prev = (r + 1) % ROWS, (r + ROWS - 1) % ROWS

    def r_x(row, d):
        return row - 2 * xi + 2 * ((xi + d) % 4)

    ordering = small[0:112]
    prior_load = pltpu.make_async_copy(prior_hbm, out, prior_sem)
    prior_load.start()

    barrier = pltpu.get_barrier_semaphore()

    def tell(row, col):
        pl.semaphore_signal(barrier, inc=1, device_id=(row, col), device_id_type=MESH)

    @pl.loop(1, ROWS)
    def _(i):
        tell((r + i) % ROWS, c)

    @pl.loop(1, COLS)
    def _(i):
        tell(r, (c + i) % COLS)

    own[...] = jnp.zeros((512, SEG), BF16)
    own[0:COEF_W, :] = design[...]
    nown[0:4, :] = small[112:116]
    nown[4:8, :] = jnp.broadcast_to(small[116:117], (4, SEG))

    pl.semaphore_wait(barrier, ROWS + COLS - 2)

    halo_copies = [
        remote(own.at[pl.ds(0, 448)], halo.at[pl.ds(0, 448)], hsend.at[0], hrecv.at[0], r_next, c),
        remote(nown, nhalo, hsend.at[1], hrecv.at[1], r_next, c),
    ]
    for copy in halo_copies:
        copy.start()

    lane = iota((1, 128), 1)
    for src in range(COLS):
        for q in range(4):
            first = COEF_W * src + 128 * q
            tile, off = first // 128, first % 128
            line = ordering[tile : tile + 1]
            if off:
                line = jnp.where(lane >= off, line, ordering[tile + 1 : tile + 2])
                line = pltpu.roll(line, 128 - off, 1)
            if q == 3:
                line = jnp.where(lane < COEF_W - 384, line, -1.0)
            slots[4 * src + q : 4 * src + q + 1] = line
    slots[128:130] = ordering[COLS * COEF_W // 128 :]

    hp = (iota((256, 128), 0) // 4).astype(F32)
    lp = iota((256, 128), 0).astype(F32)

    def factors(s):
        cc = jnp.floor((s + 0.5) * (1.0 / CSH))
        odd = cc - 2.0 * jnp.floor(cc * 0.5)
        u = s - cc * CSH + 64.0 * odd
        h = jnp.floor((u + 0.5) * (1.0 / 256.0))
        return jnp.where(s < 0.0, -1.0, 2.0 * cc + h), u - 256.0 * h

    def one_hot(row, pattern):
        return jnp.where(jnp.broadcast_to(row, pattern.shape) == pattern, 1.0, 0.0).astype(BF16)

    @pl.loop(0, GROUPS)
    def _(g):
        hi, lo = factors(slots[pl.ds(pl.multiple_of(8 * g, 8), 8), :])
        for i in range(GTILES):
            hot_hi[g, :, 128 * i : 128 * i + 128] = one_hot(hi[i : i + 1], hp)
            hot_lo[g, :, 128 * i : 128 * i + 128] = one_hot(lo[i : i + 1], lp)

    line = jnp.concatenate([small[117:118], jnp.zeros((1, SEG), F32)], 1)
    band = pltpu.roll(jnp.broadcast_to(line, (SEG, 2 * SEG)), 0, 1, stride=1, stride_axis=0)
    has_past = jnp.where(r > 0, 1.0, 0.0).astype(F32)
    band_now, band_past = band[:, :SEG], band[:, SEG:] * has_past

    def split(x):
        high = x.astype(BF16)
        return high, (x - high.astype(F32)).astype(BF16)

    now_hi, now_lo = split(band_now)
    past_hi, past_lo = split(band_past)

    for copy in halo_copies:
        copy.wait()

    mine = own[...]
    past = halo[0:448, :]
    filtered = nn(mine, now_hi) + nn(mine, now_lo)
    part = nn(past, past_hi) + nn(past, past_lo)
    filtered = jnp.concatenate([filtered[0:448] + part, filtered[448:512]], 0).astype(BF16)
    p_row, p_time = iota((512, 128), 0), iota((512, 128), 1)
    at_time = p_time == TT * (p_row // 16) + p_row % 4
    wsum = jnp.zeros((512, 128), F32)
    for q in range(4):
        pick = jnp.where(at_time & ((p_row // 4) % 4 == q), 1.0, 0.0).astype(BF16)
        wsum = wsum + nt(pick, filtered[128 * q : 128 * q + 128])
    wbuf[...] = wsum.astype(BF16).reshape(COLS, 16, 128)

    p1[c] = wbuf[c]

    @pl.loop(1, COLS)
    def _(i):
        to = (c + i) % COLS
        remote(wbuf.at[to], p1.at[c], psend.at[i], precv.at[c], r, to).start()

    n_row = iota((NUIS, SEG), 0)

    def nuisance(ref):
        v = jnp.broadcast_to(ref[0:1], (NUIS, SEG))
        for q in range(1, NPA):
            v = jnp.where(n_row % NPA == q, jnp.broadcast_to(ref[q : q + 1], (NUIS, SEG)), v)
        arc = jnp.broadcast_to(ref[4:5], (NUIS, SEG))
        return jnp.where(arc == (n_row // NPA).astype(F32), v, 0.0)

    def exact(a, b):
        return lax.dot_general(
            a, b, (((1,), (0,)), ((), ())), precision=lax.Precision.HIGHEST, preferred_element_type=F32
        )

    nfil = (exact(nuisance(nown), band_now) + exact(nuisance(nhalo), band_past)).astype(BF16)
    s_row, s_time = iota((16, 128), 0), iota((16, 128), 1)
    pick = jnp.where(s_time == TT * c + s_row % 4, 1.0, 0.0).astype(BF16)
    nhi, nlo = factors(slots[128:130, :])
    accum = jnp.zeros((256, 256), F32)
    for q in range(2):
        rep = nt(pick, nfil[128 * q : 128 * q + 128]).astype(BF16)
        x = jnp.concatenate([rep] * 16, 0) * one_hot(nhi[q : q + 1], hp)
        accum = accum + nt(x, one_hot(nlo[q : q + 1], lp))
    oacc[...] = accum

    @pl.loop(1, COLS)
    def _(i):
        src = (c + COLS - i) % COLS
        remote(wbuf.at[src], p1.at[src], psend.at[i], precv.at[src], r, src).wait()

    low4 = iota((8, 128), 0) < 4

    @pl.loop(0, GROUPS)
    def _(g):
        for k in range(2):
            msg = p1[2 * g + k].astype(F32)
            for v in range(2):
                part = msg[8 * v : 8 * v + 8]
                rot = pltpu.roll(part, 4, 0)
                for u in range(2):
                    rep = jnp.where(low4, part, rot) if u == 0 else jnp.where(low4, rot, part)
                    rep = jnp.concatenate([rep, rep], 0).astype(BF16)
                    i = 4 * k + 2 * v + u
                    lanes = slice(128 * i, 128 * i + 128)
                    xg[:, lanes] = jnp.concatenate([rep] * 16, 0) * hot_hi[g, :, lanes]
        oacc[...] += nt(xg[...], hot_lo[g])

    for cc in range(COLS):
        block = oacc[8 * cc : 8 * cc + 8]
        obuf[cc] = jnp.concatenate([block[:, :128], block[:, 128:]], 0).astype(BF16)

    @pl.loop(1, ROWS)
    def _(i):
        to = (r + i) % ROWS
        remote(obuf.at[pl.ds(2 * to, 2)], a2.at[r], asend.at[i], arecv.at[r], to, c).start()

    @pl.loop(1, COLS)
    def _(i):
        to = (c + i) % COLS
        remote(obuf.at[to], b2.at[c], bsend.at[i], brecv.at[c], r, to).start()

    a2[r] = obuf[pl.ds(2 * r, 2)]
    b2[c] = obuf[c]

    m, p = iota((448, 512), 0), iota((448, 512), 1)
    tile = 3 * ((p // 16) % 2) + 2 * ((p // 4) % 2) + (p // 8) % 2
    same = (p // 32 == (m % 64) // 4) & (p % 4 == m % 4)
    pick = jnp.where(same & (tile == m // 64), 1.0, 0.0).astype(BF16)

    @pl.loop(1, ROWS)
    def _(i):
        src = (r + ROWS - i) % ROWS
        remote(a2.at[src], a2.at[src], asend.at[i], arecv.at[src], src, c).wait()

    pieces = nn(pick, a2[...].reshape(512, 128)).astype(BF16)
    for j in range(6):
        pbuf[c, :, 128 * j : 128 * j + 128] = pieces[64 * j : 64 * j + 64]
    qbuf[c] = pieces[384:448]

    def chunk(zl, yy):
        return pbuf.at[zl * 8 + yy]

    y_of = [(y + d) % 8 for d in range(8)]
    zls = [(zl0 + k) % 4 for k in range(4)]
    sends = []

    def pass_on(k, dist, direction):
        yy = y_of[(-direction * dist) % 8]
        n = len(sends)
        copy = remote(
            chunk(zls[k], yy),
            chunk(zls[k], yy),
            gsend.at[n],
            grecv.at[zls[k] * 8 + yy],
            r,
            zl0 * 8 + y_of[direction % 8],
        )
        copy.start()
        sends.append(copy)

    def arrived(zl, yy):
        remote(chunk(zl, yy), chunk(zl, yy), gsend.at[0], grecv.at[zl * 8 + yy], r, c).wait_recv()

    qsends = []

    def q_pass(dist, direction):
        piece = qbuf.at[zl0 * 8 + y_of[(-direction * dist) % 8]]
        copy = remote(
            piece,
            piece,
            ssend.at[len(qsends)],
            srecv.at[y_of[(-direction * dist) % 8]],
            r,
            zl0 * 8 + y_of[direction % 8],
        )
        copy.start()
        qsends.append(copy)

    def q_arrived(yy):
        piece = qbuf.at[zl0 * 8 + yy]
        remote(piece, piece, ssend.at[0], srecv.at[yy], r, c).wait_recv()

    def q_step(s):
        q_arrived(y_of[-s % 8])
        if s < 4:
            q_pass(s, 1)
            q_arrived(y_of[s])
            if s < 3:
                q_pass(s, -1)

    def level_copy(dist, up):
        level = zl0 - dist if up else zl0 + dist
        levels = qbuf.at[pl.ds(8 * level, 8)]
        to = c + 8 if up else c - 8
        return remote(levels, levels, lsend.at[2 * dist + int(up)], lrecv.at[level], r, to)

    def level_goes(dist, up):
        return (zl0 >= dist) & (zl0 < 3) if up else (zl0 <= 3 - dist) & (zl0 > 0)

    def level_step(dist):
        for up in (True, False):
            if dist:
                level = zl0 - dist if up else zl0 + dist

                @pl.when(zl0 >= dist if up else zl0 <= 3 - dist)
                def _():
                    levels = qbuf.at[pl.ds(8 * level, 8)]
                    remote(levels, levels, lsend.at[0], lrecv.at[level], r, c).wait_recv()

            if dist < 3:

                @pl.when(level_goes(dist, up))
                def _():
                    level_copy(dist, up).start()

    q_pass(0, 1)
    q_pass(0, -1)
    pass_on(0, 0, 1)
    pass_on(0, 0, -1)
    for k in (1, 3, 2):
        copy = remote(
            chunk(zl0, y), chunk(zl0, y), gsend.at[len(sends)], grecv.at[c], r, zls[k] * 8 + y
        )
        copy.start()
        sends.append(copy)

    m, p = iota((512, 512), 0), iota((512, 512), 1)
    tile = 2 * ((p // 4) % 2) + (p // 8) % 2
    same = (p // 16 == (m % 128) // 4) & (p % 4 == m % 4)
    pick = jnp.where(same & (tile == m // 128), 1.0, 0.0).astype(BF16)

    @pl.loop(1, COLS)
    def _(i):
        src = (c + COLS - i) % COLS
        remote(b2.at[src], b2.at[src], bsend.at[i], brecv.at[src], r, src).wait()

    pieces = nn(pick, b2[...].reshape(512, 128)).astype(BF16)
    for j in range(4):
        bbuf[r, :, 128 * j : 128 * j + 128] = pieces[128 * j : 128 * j + 128]

    bsends = []

    def spread(row, to):
        n = len(bsends)
        copy = remote(bbuf.at[row], bbuf.at[row], qsend.at[n], qrecv.at[row], to, c)
        copy.start()
        bsends.append(copy)

    def b_arrived(row):
        remote(bbuf.at[row], bbuf.at[row], qsend.at[0], qrecv.at[row], r, c).wait_recv()

    for d in (1, 3, 2):
        spread(r, r_x(r, d))
    spread(r, r_core)

    for n, k in enumerate((1, 3, 2)):
        q_step(n + 1)
        arrived(zls[k], y)
        pass_on(k, 0, 1)
        pass_on(k, 0, -1)
    q_step(4)
    level_step(0)
    spread(r, r_z)

    def product(k, y_half):
        quad = zls[k] * 2 + y_half
        b = btr[quad, pl.ds(pl.multiple_of(64 * (c % 2), 64), CSH), :]
        out[:, :768] += nn(b, pbuf[pl.ds(4 * quad, 4)].reshape(256, 768))
        out[:, 768:] += nn(b, qbuf[pl.ds(4 * quad, 4)].reshape(256, 128))

    for s in range(1, 5):
        for k in range(4):
            right, left = (4, 3) if k % 2 == 0 else (3, 4)
            if s <= right:
                arrived(zls[k], y_of[-s % 8])
                if s < right:
                    pass_on(k, s, 1)
            if s <= left:
                arrived(zls[k], y_of[s % 8])
                if s < left:
                    pass_on(k, s, -1)
            if s == 4:
                product(k, 1 - y // 4)
        if s < 4:
            level_step(s)
        if s == 1:
            for d in (1, 3, 2):
                b_arrived(r_x(r, d))
                spread(r_x(r, d), r_core)
            b_arrived(r_z)
            for d in (1, 3, 2):
                spread(r_z, r_x(r, d))
            spread(r_z, r_core)
        if s == 2:
            for d in (1, 3, 2):
                b_arrived(r_x(r_z, d))
                spread(r_x(r_z, d), r_core)
        if s == 3:
            for base in (r, r_z):
                for d in range(4):
                    row = r_x(base, d)
                    b_arrived(row + 1 - 2 * (row % 2))
            m, p = iota((256, 256), 0), iota((256, 256), 1)
            same = (p // 16 == (m // 4) % 16) & (p % 4 == m % 4) & ((p // 4) % 4 == m // 64)
            pick = jnp.where(same, 1.0, 0.0).astype(BF16)

            @pl.loop(0, 8)
            def _(n):
                rows = bbuf[:, pl.ds(pl.multiple_of(16 * n, 16), 16), :].reshape(256, 512)
                btr[n] = nn(pick, rows).T.astype(BF16)

            prior_load.wait()
            for k in range(4):
                product(k, y // 4)

    for copy in sends + bsends + qsends:
        copy.wait_send()
    for dist in range(3):
        for up in (True, False):

            @pl.when(level_goes(dist, up))
            def _():
                level_copy(dist, up).wait_send()


def per_device(design, nuisance_vals, arc_index, filter_taps, ordering, normal_prior):
    vmem = pl.BlockSpec(memory_space=pltpu.VMEM)
    dma = pltpu.SemaphoreType.DMA
    small = jnp.concatenate(
        [
            ordering.astype(F32).reshape(112, SEG),
            nuisance_vals,
            arc_index.astype(F32).reshape(1, SEG),
            filter_taps.reshape(1, SEG),
            jnp.zeros((2, SEG), F32),
        ],
        0,
    )
    result = pl.pallas_call(
        kernel,
        out_shape=jax.ShapeDtypeStruct((CSH, RSH), F32),
        in_specs=[vmem, vmem, pl.BlockSpec(memory_space=pl.ANY)],
        out_specs=vmem,
        scratch_shapes=[
            pltpu.VMEM((136, 128), F32),
            pltpu.VMEM((512, SEG), BF16),
            pltpu.VMEM((512, SEG), BF16),
            pltpu.VMEM((8, SEG), F32),
            pltpu.VMEM((8, SEG), F32),
            pltpu.VMEM((COLS, 16, 128), BF16),
            pltpu.VMEM((COLS, 16, 128), BF16),
            pltpu.VMEM((GROUPS, 256, 128 * GTILES), BF16),
            pltpu.VMEM((GROUPS, 256, 128 * GTILES), BF16),
            pltpu.VMEM((256, 128 * GTILES), BF16),
            pltpu.VMEM((256, 256), F32),
            pltpu.VMEM((COLS, 16, 128), BF16),
            pltpu.VMEM((ROWS, 2, 16, 128), BF16),
            pltpu.VMEM((COLS, 16, 128), BF16),
            pltpu.VMEM((COLS, 64, 768), BF16),
            pltpu.VMEM((COLS, 64, 128), BF16),
            pltpu.VMEM((ROWS, SEG, 512), BF16),
            pltpu.VMEM((8, 512, 256), BF16),
            dma,
            dma((2,)),
            dma((2,)),
            dma((COLS,)),
            dma((COLS,)),
            dma((16,)),
            dma((16,)),
            dma((COLS,)),
            dma((COLS,)),
            dma((40,)),
            dma((COLS,)),
            dma((8,)),
            dma((8,)),
            dma((6,)),
            dma((4,)),
            dma((20,)),
            dma((ROWS,)),
        ],
        compiler_params=pltpu.CompilerParams(
            collective_id=0, has_side_effects=True, vmem_limit_bytes=52 * 1024 * 1024
        ),
    )(
        design.T,
        small,
        normal_prior.T,
    )
    return result.T


def solution(mesh):
    return jax.shard_map(
        per_device,
        mesh=mesh,
        in_specs=(P("row", "col"), P(None, "row"), P("row"), P(), P(), P("row", "col")),
        out_specs=P("row", "col"),
        check_vma=False,
    )
```

```python
import jax
import jax.numpy as jnp
from jax import lax
from jax.experimental import pallas as pl
from jax.experimental.pallas import tpu as pltpu
from jax.sharding import PartitionSpec as P

MESH = pl.DeviceIdType.MESH
F32, BF16 = jnp.float32, jnp.bfloat16

ROWS, COLS = 16, 32
NPA, NUIS = 4, 256
SEG = 128
COEF_W = 440
TT = 4
RSH, CSH = 896, 448
GROUPS, GTILES = 16, 8


def nt(a, b):
    return lax.dot_general(a, b, (((1,), (1,)), ((), ())), preferred_element_type=F32)


def nn(a, b):
    return lax.dot_general(a, b, (((1,), (0,)), ((), ())), preferred_element_type=F32)


def iota(shape, dim):
    return lax.broadcasted_iota(jnp.int32, shape, dim)


def remote(src, dst, send_sem, recv_sem, row, col):
    return pltpu.make_async_remote_copy(
        src_ref=src,
        dst_ref=dst,
        send_sem=send_sem,
        recv_sem=recv_sem,
        device_id=(row, col),
        device_id_type=MESH,
    )


def kernel(
    design,
    small,
    prior_hbm,
    out,
    slots,
    own,
    halo,
    nown,
    nhalo,
    wbuf,
    p1,
    hot_hi,
    hot_lo,
    xg,
    oacc,
    obuf,
    a2,
    b2,
    pbuf,
    qbuf,
    bbuf,
    btr,
    prior_sem,
    hsend,
    hrecv,
    psend,
    precv,
    asend,
    arecv,
    bsend,
    brecv,
    gsend,
    grecv,
    ssend,
    srecv,
    lsend,
    lrecv,
    qsend,
    qrecv,
):
    r, c = lax.axis_index("row"), lax.axis_index("col")
    y, zl0 = c % 8, c // 8
    xi = (r // 2) % 4
    rbase = r - 2 * xi
    r_core = r + 1 - 2 * (r % 2)
    r_z = (r + 8) % ROWS
    r_next, r_prev = (r + 1) % ROWS, (r + ROWS - 1) % ROWS

    def r_x(row, d):
        return row - 2 * xi + 2 * ((xi + d) % 4)

    ordering = small[0:112]
    prior_load = pltpu.make_async_copy(prior_hbm, out, prior_sem)
    prior_load.start()

    barrier = pltpu.get_barrier_semaphore()

    def tell(row, col):
        pl.semaphore_signal(barrier, inc=1, device_id=(row, col), device_id_type=MESH)

    @pl.loop(1, ROWS)
    def _(i):
        tell((r + i) % ROWS, c)

    @pl.loop(1, COLS)
    def _(i):
        tell(r, (c + i) % COLS)

    own[...] = jnp.zeros((512, SEG), BF16)
    own[0:COEF_W, :] = design[...]
    nown[0:4, :] = small[112:116]
    nown[4:8, :] = jnp.broadcast_to(small[116:117], (4, SEG))

    pl.semaphore_wait(barrier, ROWS + COLS - 2)

    halo_copies = [
        remote(own.at[pl.ds(0, 448)], halo.at[pl.ds(0, 448)], hsend.at[0], hrecv.at[0], r_next, c),
        remote(nown, nhalo, hsend.at[1], hrecv.at[1], r_next, c),
    ]
    for copy in halo_copies:
        copy.start()

    lane = iota((1, 128), 1)
    for src in range(COLS):
        for q in range(4):
            first = COEF_W * src + 128 * q
            tile, off = first // 128, first % 128
            line = ordering[tile : tile + 1]
            if off:
                line = jnp.where(lane >= off, line, ordering[tile + 1 : tile + 2])
                line = pltpu.roll(line, 128 - off, 1)
            if q == 3:
                line = jnp.where(lane < COEF_W - 384, line, -1.0)
            slots[4 * src + q : 4 * src + q + 1] = line
    slots[128:130] = ordering[COLS * COEF_W // 128 :]

    hp = (iota((256, 128), 0) // 4).astype(F32)
    lp = iota((256, 128), 0).astype(F32)

    def factors(s):
        cc = jnp.floor((s + 0.5) * (1.0 / CSH))
        odd = cc - 2.0 * jnp.floor(cc * 0.5)
        u = s - cc * CSH + 64.0 * odd
        h = jnp.floor((u + 0.5) * (1.0 / 256.0))
        return jnp.where(s < 0.0, -1.0, 2.0 * cc + h), u - 256.0 * h

    def one_hot(row, pattern):
        return jnp.where(jnp.broadcast_to(row, pattern.shape) == pattern, 1.0, 0.0).astype(BF16)

    @pl.loop(0, GROUPS)
    def _(g):
        hi, lo = factors(slots[pl.ds(pl.multiple_of(8 * g, 8), 8), :])
        for i in range(GTILES):
            hot_hi[g, :, 128 * i : 128 * i + 128] = one_hot(hi[i : i + 1], hp)
            hot_lo[g, :, 128 * i : 128 * i + 128] = one_hot(lo[i : i + 1], lp)

    line = jnp.concatenate([small[117:118], jnp.zeros((1, SEG), F32)], 1)
    band = pltpu.roll(jnp.broadcast_to(line, (SEG, 2 * SEG)), 0, 1, stride=1, stride_axis=0)
    has_past = jnp.where(r > 0, 1.0, 0.0).astype(F32)
    band_now, band_past = band[:, :SEG], band[:, SEG:] * has_past

    def split(x):
        high = x.astype(BF16)
        return high, (x - high.astype(F32)).astype(BF16)

    now_hi, now_lo = split(band_now)
    past_hi, past_lo = split(band_past)

    for copy in halo_copies:
        copy.wait()

    mine = own[...]
    past = halo[0:448, :]
    filtered = nn(mine, now_hi) + nn(mine, now_lo)
    part = nn(past, past_hi) + nn(past, past_lo)
    filtered = jnp.concatenate([filtered[0:448] + part, filtered[448:512]], 0).astype(BF16)
    p_row, p_time = iota((512, 128), 0), iota((512, 128), 1)
    at_time = p_time == TT * (p_row // 16) + p_row % 4
    wsum = jnp.zeros((512, 128), F32)
    for q in range(4):
        pick = jnp.where(at_time & ((p_row // 4) % 4 == q), 1.0, 0.0).astype(BF16)
        wsum = wsum + nt(pick, filtered[128 * q : 128 * q + 128])
    wbuf[...] = wsum.astype(BF16).reshape(COLS, 16, 128)

    p1[c] = wbuf[c]

    @pl.loop(1, COLS)
    def _(i):
        to = (c + i) % COLS
        remote(wbuf.at[to], p1.at[c], psend.at[i], precv.at[c], r, to).start()

    n_row = iota((NUIS, SEG), 0)

    def nuisance(ref):
        v = jnp.broadcast_to(ref[0:1], (NUIS, SEG))
        for q in range(1, NPA):
            v = jnp.where(n_row % NPA == q, jnp.broadcast_to(ref[q : q + 1], (NUIS, SEG)), v)
        arc = jnp.broadcast_to(ref[4:5], (NUIS, SEG))
        return jnp.where(arc == (n_row // NPA).astype(F32), v, 0.0)

    def exact(a, b):
        return lax.dot_general(
            a, b, (((1,), (0,)), ((), ())), precision=lax.Precision.HIGHEST, preferred_element_type=F32
        )

    nfil = (exact(nuisance(nown), band_now) + exact(nuisance(nhalo), band_past)).astype(BF16)
    s_row, s_time = iota((16, 128), 0), iota((16, 128), 1)
    pick = jnp.where(s_time == TT * c + s_row % 4, 1.0, 0.0).astype(BF16)
    nhi, nlo = factors(slots[128:130, :])
    accum = jnp.zeros((256, 256), F32)
    for q in range(2):
        rep = nt(pick, nfil[128 * q : 128 * q + 128]).astype(BF16)
        x = jnp.concatenate([rep] * 16, 0) * one_hot(nhi[q : q + 1], hp)
        accum = accum + nt(x, one_hot(nlo[q : q + 1], lp))
    oacc[...] = accum

    @pl.loop(1, COLS)
    def _(i):
        src = (c + COLS - i) % COLS
        remote(wbuf.at[src], p1.at[src], psend.at[i], precv.at[src], r, src).wait()

    low4 = iota((8, 128), 0) < 4

    @pl.loop(0, GROUPS)
    def _(g):
        for k in range(2):
            msg = p1[2 * g + k].astype(F32)
            for v in range(2):
                part = msg[8 * v : 8 * v + 8]
                rot = pltpu.roll(part, 4, 0)
                for u in range(2):
                    rep = jnp.where(low4, part, rot) if u == 0 else jnp.where(low4, rot, part)
                    rep = jnp.concatenate([rep, rep], 0).astype(BF16)
                    i = 4 * k + 2 * v + u
                    lanes = slice(128 * i, 128 * i + 128)
                    xg[:, lanes] = jnp.concatenate([rep] * 16, 0) * hot_hi[g, :, lanes]
        oacc[...] += nt(xg[...], hot_lo[g])

    for cc in range(COLS):
        block = oacc[8 * cc : 8 * cc + 8]
        obuf[cc] = jnp.concatenate([block[:, :128], block[:, 128:]], 0).astype(BF16)

    @pl.loop(1, ROWS)
    def _(i):
        to = (r + i) % ROWS
        remote(obuf.at[pl.ds(2 * to, 2)], a2.at[r], asend.at[i], arecv.at[r], to, c).start()

    @pl.loop(1, COLS)
    def _(i):
        to = (c + i) % COLS
        remote(obuf.at[to], b2.at[c], bsend.at[i], brecv.at[c], r, to).start()

    a2[r] = obuf[pl.ds(2 * r, 2)]
    b2[c] = obuf[c]

    m, p = iota((448, 512), 0), iota((448, 512), 1)
    tile = 3 * ((p // 16) % 2) + 2 * ((p // 4) % 2) + (p // 8) % 2
    same = (p // 32 == (m % 64) // 4) & (p % 4 == m % 4)
    pick = jnp.where(same & (tile == m // 64), 1.0, 0.0).astype(BF16)

    @pl.loop(1, ROWS)
    def _(i):
        src = (r + ROWS - i) % ROWS
        remote(a2.at[src], a2.at[src], asend.at[i], arecv.at[src], src, c).wait()

    pieces = nn(pick, a2[...].reshape(512, 128)).astype(BF16)
    for j in range(6):
        pbuf[c, :, 128 * j : 128 * j + 128] = pieces[64 * j : 64 * j + 64]
    qbuf[c] = pieces[384:448]

    def chunk(zl, yy):
        return pbuf.at[zl * 8 + yy]

    y_of = [(y + d) % 8 for d in range(8)]
    zls = [(zl0 + k) % 4 for k in range(4)]
    sends = []

    def pass_on(k, dist, direction):
        yy = y_of[(-direction * dist) % 8]
        n = len(sends)
        copy = remote(
            chunk(zls[k], yy),
            chunk(zls[k], yy),
            gsend.at[n],
            grecv.at[zls[k] * 8 + yy],
            r,
            zl0 * 8 + y_of[direction % 8],
        )
        copy.start()
        sends.append(copy)

    def arrived(zl, yy):
        remote(chunk(zl, yy), chunk(zl, yy), gsend.at[0], grecv.at[zl * 8 + yy], r, c).wait_recv()

    qsends = []

    def q_pass(dist, direction):
        piece = qbuf.at[zl0 * 8 + y_of[(-direction * dist) % 8]]
        copy = remote(
            piece,
            piece,
            ssend.at[len(qsends)],
            srecv.at[y_of[(-direction * dist) % 8]],
            r,
            zl0 * 8 + y_of[direction % 8],
        )
        copy.start()
        qsends.append(copy)

    def q_arrived(yy):
        piece = qbuf.at[zl0 * 8 + yy]
        remote(piece, piece, ssend.at[0], srecv.at[yy], r, c).wait_recv()

    def q_step(s):
        q_arrived(y_of[-s % 8])
        if s < 4:
            q_pass(s, 1)
            q_arrived(y_of[s])
            if s < 3:
                q_pass(s, -1)

    def level_copy(dist, up):
        level = zl0 - dist if up else zl0 + dist
        levels = qbuf.at[pl.ds(8 * level, 8)]
        to = c + 8 if up else c - 8
        return remote(levels, levels, lsend.at[2 * dist + int(up)], lrecv.at[level], r, to)

    def level_goes(dist, up):
        return (zl0 >= dist) & (zl0 < 3) if up else (zl0 <= 3 - dist) & (zl0 > 0)

    def level_step(dist):
        for up in (True, False):
            if dist:
                level = zl0 - dist if up else zl0 + dist

                @pl.when(zl0 >= dist if up else zl0 <= 3 - dist)
                def _():
                    levels = qbuf.at[pl.ds(8 * level, 8)]
                    remote(levels, levels, lsend.at[0], lrecv.at[level], r, c).wait_recv()

            if dist < 3:

                @pl.when(level_goes(dist, up))
                def _():
                    level_copy(dist, up).start()

    q_pass(0, 1)
    q_pass(0, -1)
    pass_on(0, 0, 1)
    pass_on(0, 0, -1)
    for k in (1, 3, 2):
        copy = remote(
            chunk(zl0, y), chunk(zl0, y), gsend.at[len(sends)], grecv.at[c], r, zls[k] * 8 + y
        )
        copy.start()
        sends.append(copy)

    m, p = iota((512, 512), 0), iota((512, 512), 1)
    tile = 2 * ((p // 4) % 2) + (p // 8) % 2
    same = (p // 16 == (m % 128) // 4) & (p % 4 == m % 4)
    pick = jnp.where(same & (tile == m // 128), 1.0, 0.0).astype(BF16)

    @pl.loop(1, COLS)
    def _(i):
        src = (c + COLS - i) % COLS
        remote(b2.at[src], b2.at[src], bsend.at[i], brecv.at[src], r, src).wait()

    pieces = nn(pick, b2[...].reshape(512, 128)).astype(BF16)
    for j in range(4):
        bbuf[r, :, 128 * j : 128 * j + 128] = pieces[128 * j : 128 * j + 128]

    bsends = []

    def spread(row, to):
        n = len(bsends)
        copy = remote(bbuf.at[row], bbuf.at[row], qsend.at[n], qrecv.at[row], to, c)
        copy.start()
        bsends.append(copy)

    def b_arrived(row):
        remote(bbuf.at[row], bbuf.at[row], qsend.at[0], qrecv.at[row], r, c).wait_recv()

    for d in (1, 3, 2):
        spread(r, r_x(r, d))
    spread(r, r_core)

    for n, k in enumerate((1, 3, 2)):
        q_step(n + 1)
        arrived(zls[k], y)
        pass_on(k, 0, 1)
        pass_on(k, 0, -1)
    spread(r, r_z)
    q_step(4)
    level_step(0)

    def product(k, y_half):
        quad = zls[k] * 2 + y_half
        b = btr[quad, pl.ds(pl.multiple_of(64 * (c % 2), 64), CSH), :]
        out[:, :768] += nn(b, pbuf[pl.ds(4 * quad, 4)].reshape(256, 768))
        out[:, 768:] += nn(b, qbuf[pl.ds(4 * quad, 4)].reshape(256, 128))

    for s in range(1, 5):
        for k in range(4):
            right, left = (4, 3) if k % 2 == 0 else (3, 4)
            if s <= right:
                arrived(zls[k], y_of[-s % 8])
                if s < right:
                    pass_on(k, s, 1)
            if s <= left:
                arrived(zls[k], y_of[s % 8])
                if s < left:
                    pass_on(k, s, -1)
            if s == 4:
                product(k, 1 - y // 4)
        if s < 4:
            level_step(s)
        if s == 1:
            for d in (1, 3, 2):
                b_arrived(r_x(r, d))
                spread(r_x(r, d), r_core)
            b_arrived(r_z)
            for d in (1, 3, 2):
                spread(r_z, r_x(r, d))
            spread(r_z, r_core)
        if s == 2:
            for d in (1, 3, 2):
                b_arrived(r_x(r_z, d))
                spread(r_x(r_z, d), r_core)
        if s == 3:
            for base in (r, r_z):
                for d in range(4):
                    row = r_x(base, d)
                    b_arrived(row + 1 - 2 * (row % 2))
            m, p = iota((256, 256), 0), iota((256, 256), 1)
            same = (p // 16 == (m // 4) % 16) & (p % 4 == m % 4) & ((p // 4) % 4 == m // 64)
            pick = jnp.where(same, 1.0, 0.0).astype(BF16)

            @pl.loop(0, 8)
            def _(n):
                rows = bbuf[:, pl.ds(pl.multiple_of(16 * n, 16), 16), :].reshape(256, 512)
                btr[n] = nn(pick, rows).T.astype(BF16)

            prior_load.wait()
            for k in range(4):
                product(k, y // 4)

    for copy in sends + bsends + qsends:
        copy.wait_send()
    for dist in range(3):
        for up in (True, False):

            @pl.when(level_goes(dist, up))
            def _():
                level_copy(dist, up).wait_send()


def per_device(design, nuisance_vals, arc_index, filter_taps, ordering, normal_prior):
    vmem = pl.BlockSpec(memory_space=pltpu.VMEM)
    dma = pltpu.SemaphoreType.DMA
    small = jnp.concatenate(
        [
            ordering.astype(F32).reshape(112, SEG),
            nuisance_vals,
            arc_index.astype(F32).reshape(1, SEG),
            filter_taps.reshape(1, SEG),
            jnp.zeros((2, SEG), F32),
        ],
        0,
    )
    result = pl.pallas_call(
        kernel,
        out_shape=jax.ShapeDtypeStruct((CSH, RSH), F32),
        in_specs=[vmem, vmem, pl.BlockSpec(memory_space=pl.ANY)],
        out_specs=vmem,
        scratch_shapes=[
            pltpu.VMEM((136, 128), F32),
            pltpu.VMEM((512, SEG), BF16),
            pltpu.VMEM((512, SEG), BF16),
            pltpu.VMEM((8, SEG), F32),
            pltpu.VMEM((8, SEG), F32),
            pltpu.VMEM((COLS, 16, 128), BF16),
            pltpu.VMEM((COLS, 16, 128), BF16),
            pltpu.VMEM((GROUPS, 256, 128 * GTILES), BF16),
            pltpu.VMEM((GROUPS, 256, 128 * GTILES), BF16),
            pltpu.VMEM((256, 128 * GTILES), BF16),
            pltpu.VMEM((256, 256), F32),
            pltpu.VMEM((COLS, 16, 128), BF16),
            pltpu.VMEM((ROWS, 2, 16, 128), BF16),
            pltpu.VMEM((COLS, 16, 128), BF16),
            pltpu.VMEM((COLS, 64, 768), BF16),
            pltpu.VMEM((COLS, 64, 128), BF16),
            pltpu.VMEM((ROWS, SEG, 512), BF16),
            pltpu.VMEM((8, 512, 256), BF16),
            dma,
            dma((2,)),
            dma((2,)),
            dma((COLS,)),
            dma((COLS,)),
            dma((16,)),
            dma((16,)),
            dma((COLS,)),
            dma((COLS,)),
            dma((40,)),
            dma((COLS,)),
            dma((8,)),
            dma((8,)),
            dma((6,)),
            dma((4,)),
            dma((20,)),
            dma((ROWS,)),
        ],
        compiler_params=pltpu.CompilerParams(
            collective_id=0, has_side_effects=True, vmem_limit_bytes=52 * 1024 * 1024
        ),
    )(
        design.T,
        small,
        normal_prior.T,
    )
    return result.T


def solution(mesh):
    return jax.shard_map(
        per_device,
        mesh=mesh,
        in_specs=(P("row", "col"), P(None, "row"), P("row"), P(), P(), P("row", "col")),
        out_specs=P("row", "col"),
        check_vma=False,
    )
```
